128 devices in a mesh: section: 2 (over x_hi), replica: 16 (over z, y), tensor: 4 (over x_lo, core).
Axes of the slice: x: 4 (x_hi: 2, x_lo: 2; x = x_hi * 2 + x_lo), y: 4, z: 4, core: 2. Of those that a mesh axis runs over, the one named last changes fastest.
Arguments:
- inner_input: bfloat16 [3, 512, 8192], P(None, 'replica', 'tensor'), may hold values from -6 to 6
- gate_input: bfloat16 [3, 512, 8192], P(None, 'replica', 'tensor'), may hold values from -6 to 6
- residual: bfloat16 [3, 512, 4096], P(None, 'replica'), may hold values from -24 to 24
- projection: bfloat16 [2, 8192, 4096], P('section', 'tensor'), may hold values from -0.0625 to 0.0625
- state_proj: bfloat16 [2, 8192, 288], P('section', 'tensor'), may hold values from -0.0625 to 0.0625
- step_proj: bfloat16 [2, 256, 8192], P('section', None, 'tensor'), may hold values from -0.375 to 0.375
- conv_weight: float32 [2, 4, 8192], P('section', None, 'tensor'), may hold values from -3 to 3
- conv_bias: float32 [2, 8192], P('section', 'tensor'), may hold values from -3 to 3
- decay_rate: float32 [2, 16, 8192], P('section', None, 'tensor'), may hold values from 1 to 16
- skip_gain: float32 [2, 8192], P('section', 'tensor'), may hold values from 0.5 to 1.5
- step_bias: float32 [2, 8192], P('section', 'tensor'), may hold values from -4 to -1
- norm_gain: bfloat16 [4096], replicated, may hold values from 0.099609375 to 1.8984375
- state_codes: bfloat16 [2, 512, 16, 8192], P('section', 'replica', None, 'tensor'), may hold values from -4 to 4
- state_scales: bfloat16 [2, 512, 64], P('section', 'replica', 'tensor'), may hold values from 0.19921875 to 2
- conv_window: bfloat16 [2, 512, 3, 8192], P('section', 'replica', None, 'tensor'), may hold values from -6 to 6
- cache_codes: bfloat16 [2, 64, 16, 8192], P('section', 'replica', None, 'tensor'), may hold values from -4 to 4
- cache_scales: bfloat16 [2, 64, 64], P('section', 'replica', 'tensor'), may hold values from 0.19921875 to 2
- cache_window: bfloat16 [2, 64, 3, 8192], P('section', 'replica', None, 'tensor'), may hold values from -6 to 6
- finished: int32 [3, 512], P(None, 'replica'), may hold values from 0 to 1
- refill_source: int32 [3, 512], replicated, may hold values from -1 to 63, as said below
Outputs:
- stream_out: bfloat16 [3, 512, 4096], P(None, 'replica', 'tensor')
- scan_out: bfloat16 [2, 3, 512, 8192], P('section', None, 'replica', 'tensor')
- codes_out: bfloat16 [2, 512, 16, 8192], P('section', 'replica', None, 'tensor')
- scales_out: bfloat16 [2, 512, 64], P('section', 'replica', 'tensor')
- window_out: bfloat16 [2, 512, 3, 8192], P('section', 'replica', None, 'tensor')
The draws below stay inside these ranges and needn't reach their ends.
Inputs may be any that keep to these rules, and one draw needn't show every extreme that they name: `refill_source`: -1 wherever finished is 0. A row index r >= 0 lies on replica r // 4. In each tick at most 2 slots of one replica take rows that lie on one replica, and at most 23 slots of one replica take rows; both bounds are reached in every tick.
All inputs are finite; a program needn't handle non-finite values.
Results may differ from the reference program's by a relative error of at most 0.025.
Values may be sent and summed in bfloat16 or wider, within the bound.
No kernel may reach another device: no remote copies, remote signals or barrier semaphores. Data moves between devices by JAX's collectives and lax.ppermute only.
A program may use at most 128 MiB of HBM per device.

```python
import math
import jax
import jax.numpy as jnp
from jax import lax

D = 4096
INNER = 8192
RANK = 256
STATES = 16
CONV = 4
BLOCK = 128
TICKS = 3
SLOTS_DEV = 32
POOL_DEV = 4
SLOTS = 512
POOL = 64
CAP = 2


def refill_plan(key):
    replicas = SLOTS // SLOTS_DEV
    lowest = max(SLOTS_DEV // 4, CAP + 2)
    highest = 3 * SLOTS_DEV // 4
    key_list = jax.random.split(key, 6)
    perm_keys = jax.random.split(key_list[0], TICKS * replicas)
    ranking = jax.vmap(lambda single: jax.random.permutation(single, SLOTS_DEV))(perm_keys).reshape(TICKS, replicas, SLOTS_DEV)
    tallies = jax.random.randint(key_list[1], (TICKS, replicas), lowest, highest + 1)
    busiest = jax.random.randint(key_list[2], (TICKS, 1), 0, replicas)
    chosen = jnp.arange(replicas)[None, :] == busiest
    tallies = jnp.where(chosen, highest, tallies)
    unfilled = jnp.where(chosen, 1, jax.random.randint(key_list[3], (TICKS, replicas), 1, 3))
    shifts = jax.random.randint(key_list[4], (TICKS, replicas), 0, replicas)
    within = jax.random.randint(key_list[5], (TICKS, replicas, SLOTS_DEV), 0, POOL_DEV)
    ended = ranking < tallies[:, :, None]
    filled = ranking < (tallies - unfilled)[:, :, None]
    source = (jnp.arange(replicas)[None, :, None] + 1 + shifts[:, :, None] + ranking // CAP) % replicas
    sources = jnp.where(filled, source * POOL_DEV + within, -1)
    return (ended.astype(jnp.int32).reshape(TICKS, SLOTS), sources.astype(jnp.int32).reshape(TICKS, SLOTS))


def draw_finished(key, part):
    ended, sources = refill_plan(key)
    return ended


def draw_refill_source(key, part):
    ended, sources = refill_plan(key)
    return sources


def draw_residual(key, part):
    key = jax.random.fold_in(key, 3)
    base_key, row_key, col_key = jax.random.split(key, 3)
    shape_all = (TICKS, SLOTS, D)
    base_values = jnp.clip(jax.random.normal(base_key, shape_all, jnp.float32), -4.0, 4.0)
    row_scale = jnp.exp(jax.random.uniform(row_key, (TICKS, SLOTS, 1), jnp.float32, math.log(0.2), math.log(2.0)))
    col_scale = jnp.exp(jax.random.uniform(col_key, (1, 1, D), jnp.float32, math.log(0.3), math.log(3.0)))
    return (base_values * row_scale * col_scale).astype(jnp.bfloat16)


def levels(own_key, shape, shards, least, top_value):
    gain, own = 1.0, jax.random.fold_in(own_key, 6)
    for position, blocks in shards:
        draws = jnp.exp(jax.random.uniform(jax.random.fold_in(own, position), (blocks,), jnp.float32, least / len(shards), top_value / len(shards)))
        gain = gain * jnp.repeat(draws, shape[position] // blocks).reshape([-1 if axis == position else 1 for axis in range(len(shape))])
    return gain


def noise(rng, dims, scale, bound, cuts=(), dtype=jnp.bfloat16):
    values = jax.random.normal(rng, dims, jnp.float32) * scale
    if len(cuts) > 0:
        values = levels(rng, dims, cuts, -0.22, 0.18) * values
    return jnp.clip(values, min=-bound, max=bound).astype(dtype)


def setup_inputs(seed: int = 0) -> dict:
    seeds = jax.random.split(jax.random.key(seed), 21)
    return {
        "inner_input": noise(seeds[0], (TICKS, SLOTS, INNER), 1.0, 6.0, ((1, 16), (2, 4))),
        "gate_input": noise(seeds[1], (TICKS, SLOTS, INNER), 1.0, 6.0, ((1, 16), (2, 4))),
        "residual": draw_residual(jax.random.fold_in(seeds[20], 71), 0),
        "projection": noise(seeds[3], (2, INNER, D), INNER ** -0.5, 0.0625, ((0, 2), (1, 4))),
        "state_proj": noise(seeds[4], (2, INNER, RANK + 2 * STATES), INNER ** -0.5, 0.0625, ((0, 2), (1, 4))),
        "step_proj": noise(seeds[5], (2, RANK, INNER), RANK ** -0.5, 0.375, ((0, 2), (2, 4))),
        "conv_weight": noise(seeds[6], (2, CONV, INNER), 0.5, 3.0, ((0, 2), (2, 4)), jnp.float32),
        "conv_bias": noise(seeds[7], (2, INNER), 0.3, 3.0, ((0, 2), (1, 4)), jnp.float32),
        "decay_rate": jnp.clip(jnp.exp(math.log(16.0) - 2.7725887 * jax.random.uniform(seeds[8], (2, STATES, INNER), jnp.float32) ** levels(seeds[8], (2, STATES, INNER), ((0, 2), (2, 4)), -0.2, 0.2)), 1.0, 16.0),
        "skip_gain": jnp.clip(0.5 + 1.0 * jax.random.uniform(seeds[9], (2, INNER), jnp.float32) ** levels(seeds[9], (2, INNER), ((0, 2), (1, 4)), -0.2, 0.2), 0.5, 1.5),
        "step_bias": jnp.clip(-4.0 + 3.0 * jax.random.uniform(seeds[10], (2, INNER), jnp.float32) ** levels(seeds[10], (2, INNER), ((0, 2), (1, 4)), -0.2, 0.2), -4.0, -1.0),
        "norm_gain": jnp.clip(1.0 + 0.18 * jax.random.normal(seeds[11], (D,), jnp.float32), 0.099609375, 1.8984375).astype(jnp.bfloat16),
        "state_codes": noise(seeds[12], (2, SLOTS, STATES, INNER), 1.0, 4.0, ((0, 2), (1, 16), (3, 4))),
        "state_scales": jnp.clip(jnp.exp(math.log(2.0) - 2.306499 * jax.random.uniform(seeds[13], (2, SLOTS, INNER // BLOCK), jnp.float32) ** levels(seeds[13], (2, SLOTS, INNER // BLOCK), ((0, 2), (1, 16), (2, 4)), -0.2, 0.2)), 0.19921875, 2.0).astype(jnp.bfloat16),
        "conv_window": noise(seeds[14], (2, SLOTS, CONV - 1, INNER), 1.0, 6.0, ((0, 2), (1, 16), (3, 4))),
        "cache_codes": noise(seeds[15], (2, POOL, STATES, INNER), 1.0, 4.0, ((0, 2), (1, 16), (3, 4))),
        "cache_scales": jnp.clip(jnp.exp(math.log(2.0) - 2.306499 * jax.random.uniform(seeds[16], (2, POOL, INNER // BLOCK), jnp.float32) ** levels(seeds[16], (2, POOL, INNER // BLOCK), ((0, 2), (1, 16), (2, 4)), -0.2, 0.2)), 0.19921875, 2.0).astype(jnp.bfloat16),
        "cache_window": noise(seeds[17], (2, POOL, CONV - 1, INNER), 1.0, 6.0, ((0, 2), (1, 16), (3, 4))),
        "finished": draw_finished(jax.random.fold_in(seeds[20], 71), 0),
        "refill_source": draw_refill_source(jax.random.fold_in(seeds[20], 71), 0),
    }


def scan_update(conv_out, projected, inputs, quant_codes, quant_scales, past_inputs, step_proj, step_bias, decay_rate, skip_gain):
    step_low = projected[:, :RANK].astype(jnp.bfloat16)
    step_size = jax.nn.softplus(jnp.dot(step_low, step_proj, preferred_element_type=jnp.float32) + step_bias)
    entry_gain = projected[:, RANK:RANK + STATES]
    readout = projected[:, RANK + STATES:]
    expanded = jnp.repeat(quant_scales.astype(jnp.float32), BLOCK, axis=-1)[:, None, :]
    previous = quant_codes.astype(jnp.float32) * expanded
    state_new = jnp.exp(-step_size[:, None, :] * decay_rate[None]) * previous + (step_size * conv_out)[:, None, :] * entry_gain[:, :, None]
    output = lax.optimization_barrier(jnp.sum(readout[:, :, None] * state_new, axis=1)) + skip_gain * conv_out
    row_count = state_new.shape[0]
    blocked = state_new.reshape(row_count, STATES, -1, BLOCK)
    new_scales = jnp.sqrt(lax.optimization_barrier(jnp.mean(blocked * blocked, axis=(1, 3))) + 1e-06).astype(jnp.bfloat16)
    divisor = jnp.repeat(new_scales.astype(jnp.float32), BLOCK, axis=-1)[:, None, :]
    new_codes = (state_new / divisor).astype(jnp.bfloat16)
    new_window = jnp.concatenate([past_inputs[:, 1:], inputs[:, None, :]], axis=1)
    return (output, new_codes, new_scales, new_window)

def run_mixer(inputs, quant_codes, quant_scales, past_inputs, conv_weight, conv_bias, state_proj, step_proj, step_bias, decay_rate, skip_gain):
    stacked = jnp.concatenate([past_inputs, inputs[:, None, :]], axis=1).astype(jnp.float32)
    conv_out = jax.nn.silu(lax.optimization_barrier(jnp.sum(stacked * conv_weight[None], axis=1)) + conv_bias)
    projected = jnp.dot(conv_out.astype(jnp.bfloat16), state_proj, preferred_element_type=jnp.float32)
    return scan_update(conv_out, projected, inputs, quant_codes, quant_scales, past_inputs, step_proj, step_bias, decay_rate, skip_gain)

def apply_refill(states, done_row, source_row, cached):
    present = source_row >= 0
    picked = jnp.where(present, source_row, 0)
    result = []
    for current, table in zip(states, cached):
        tail_shape = (1,) * (current.ndim - 1)
        take_mask = ((done_row == 1) & present).reshape((-1,) + tail_shape)
        zero_mask = (done_row == 1).reshape((-1,) + tail_shape)
        fetched = table[picked]
        result.append(jnp.where(take_mask, fetched, jnp.where(zero_mask, jnp.zeros_like(current), current)))
    return result

def reference(inner_input, gate_input, residual, projection, state_proj, step_proj, conv_weight, conv_bias, decay_rate, skip_gain, step_bias, norm_gain, state_codes, state_scales, conv_window, cache_codes, cache_scales, cache_window, finished, refill_source):
    layers = [[state_codes[0], state_scales[0], conv_window[0]], [state_codes[1], state_scales[1], conv_window[1]]]
    streams = []
    scanned = [[], []]
    for tick_index in range(TICKS):
        inputs = inner_input[tick_index]
        for layer_index in range(2):
            output, new_codes, new_scales, new_window = run_mixer(inputs, layers[layer_index][0], layers[layer_index][1], layers[layer_index][2], conv_weight[layer_index], conv_bias[layer_index], state_proj[layer_index], step_proj[layer_index], step_bias[layer_index], decay_rate[layer_index], skip_gain[layer_index])
            scanned[layer_index].append(output.astype(jnp.bfloat16))
            if layer_index == 0:
                gated = (output * jax.nn.silu(gate_input[tick_index].astype(jnp.float32))).astype(jnp.bfloat16)
                mixed = jnp.dot(gated, projection[0], preferred_element_type=jnp.float32)
                stream = (residual[tick_index].astype(jnp.float32) + mixed).astype(jnp.bfloat16)
                streams.append(stream)
                values = stream.astype(jnp.float32)
                normed = (values * lax.rsqrt(lax.optimization_barrier(jnp.mean(values * values, axis=-1, keepdims=True)) + 1e-05) * norm_gain.astype(jnp.float32)).astype(jnp.bfloat16)
                inputs = jnp.dot(normed, projection[1].T, preferred_element_type=jnp.float32).astype(jnp.bfloat16)
            cached = (cache_codes[layer_index], cache_scales[layer_index], cache_window[layer_index])
            layers[layer_index] = apply_refill((new_codes, new_scales, new_window), finished[tick_index], refill_source[tick_index], cached)
    stream_out = jnp.stack(streams)
    scan_out = jnp.stack([jnp.stack(scanned[0]), jnp.stack(scanned[1])])
    codes_out = jnp.stack([layers[0][0], layers[1][0]])
    scales_out = jnp.stack([layers[0][1], layers[1][1]])
    window_out = jnp.stack([layers[0][2], layers[1][2]])
    return (stream_out, scan_out, codes_out, scales_out, window_out)
```

```python
import functools
import math

import jax
import jax.numpy as jnp
from jax import lax
from jax.experimental import pallas as pl
from jax.experimental.pallas import tpu as pltpu
from jax.sharding import PartitionSpec as P

RANK = 256
STATES = 16
TICKS = 3
SLOTS = 32
ROWS = TICKS * SLOTS
CHANNELS = 2048
FEATURES = 4096
SHARE = FEATURES // 4
CB = 256
STEPS = CHANNELS // CB
LANES = 128
TERMS = RANK + 2 * STATES
POOL = 64
LOG2E = math.log2(math.e)
F32 = jnp.float32
BF16 = jnp.bfloat16
MIB = 1024 * 1024


def cat_kernel(a, b, c, d, out):
    out[...] = jnp.concatenate([a[...], b[...], c[...], d[...]], axis=0)


def cat_rows(pieces):
    rows, lanes = pieces[0].shape
    return pl.pallas_call(
        cat_kernel,
        out_shape=jax.ShapeDtypeStruct((4 * rows, lanes), BF16),
        name="cat_rows",
    )(*pieces)


def silu(x):
    return x / (1.0 + jnp.exp(-x))


def softplus(x):
    return jnp.maximum(x, 0.0) + jnp.log1p(jnp.exp(-jnp.abs(x)))


def conv_block(inputs, win, cached, onehot, masks, weight, bias):
    fetched = jnp.dot(onehot, cached, preferred_element_type=F32)
    past = [win[k].astype(F32) for k in range(3)]
    outs = []
    for tick in range(TICKS):
        rows = slice(tick * SLOTS, (tick + 1) * SLOTS)
        now = inputs[rows].astype(F32)
        taps = past + [now]
        total = bias
        for k in range(4):
            total = total + weight[k : k + 1] * taps[k]
        outs.append(silu(total))
        mask = masks[rows, :1] > 0.5
        past = [
            jnp.where(mask, fetched[rows, k * CB : (k + 1) * CB], taps[k + 1]) for k in range(3)
        ]
    return jnp.concatenate(outs, axis=0), past


def conv_kernel(
    inputs, win, c0, c1, c2, c3, onehot, masks, weight, bias, proj, conv_out, terms, acc
):
    step = pl.program_id(0)
    cached = jnp.concatenate([c0[...], c1[...], c2[...], c3[...]], axis=0)
    conv, _ = conv_block(
        inputs[...], win, cached, onehot[...], masks[...], weight[...], bias[...]
    )
    conv_out[...] = conv
    part = jnp.dot(conv.astype(BF16), proj[...], preferred_element_type=F32)

    @pl.when(step == 0)
    def _():
        acc[...] = part

    @pl.when(step > 0)
    def _():
        acc[...] += part

    @pl.when(step == STEPS - 1)
    def _():
        terms[...] = acc[...].astype(BF16)


def full(shape):
    return pl.BlockSpec(shape, lambda j, *_: (0,) * len(shape))


def columns(rows, width=CB):
    return pl.BlockSpec((rows, width), lambda j, *_: (0, j))


def conv_call(inputs, win, pieces, onehot, masks, weight, bias, proj):
    return pl.pallas_call(
        conv_kernel,
        grid=(STEPS,),
        in_specs=[
            columns(ROWS),
            pl.BlockSpec((3, SLOTS, CB), lambda j: (0, 0, j)),
            *[columns(16, 3 * CB)] * 4,
            full((ROWS, POOL)),
            full((ROWS, LANES)),
            columns(4),
            columns(1),
            pl.BlockSpec((CB, TERMS), lambda j: (j, 0)),
        ],
        out_specs=[columns(ROWS), full((ROWS, TERMS))],
        out_shape=[
            jax.ShapeDtypeStruct((ROWS, CHANNELS), F32),
            jax.ShapeDtypeStruct((ROWS, TERMS), BF16),
        ],
        scratch_shapes=[pltpu.VMEM((ROWS, TERMS), F32)],
        compiler_params=pltpu.CompilerParams(vmem_limit_bytes=32 * MIB),
        name="conv_terms",
    )(inputs, win, *pieces, onehot, masks, weight, bias, proj)


def project_kernel(
    where,
    s_own,
    s_a,
    s_b,
    s_c,
    first,
    gain,
    big,
    inputs,
    win,
    c0,
    c1,
    c2,
    c3,
    onehot,
    masks,
    weight,
    bias,
    proj,
    conv_out,
    terms,
    win_out,
    stream_out,
    acc,
    values,
    normed,
    entering,
):
    step = pl.program_id(0)
    section, column = where[0], where[1]

    @pl.when((step == 0) & (section == 0))
    def _():
        stream_out[...] = first[...]

    @pl.when((step == 0) & (section == 1))
    def _():
        values[column ^ 2] = s_own[...]
        values[column] = s_a[...]
        values[column ^ 3] = s_b[...]
        values[column ^ 1] = s_c[...]
        stream_out[...] = s_a[...]
        total = jnp.zeros((ROWS, 1), F32)
        for f in range(4):
            v = values[f].astype(F32)
            total = total + jnp.sum(v * v, axis=1, keepdims=True)
        factor = lax.rsqrt(total * (1.0 / FEATURES) + 1e-05)
        for f in range(4):
            cols = slice(f * SHARE, (f + 1) * SHARE)
            v = values[f].astype(F32)
            normed[:, cols] = (v * factor * gain[:, cols].astype(F32)).astype(BF16)

    @pl.when(section == 1)
    def _():
        entering[...] = lax.dot_general(
            normed[...], big[...], (((1,), (1,)), ((), ())), preferred_element_type=F32
        ).astype(BF16)

    @pl.when(section == 0)
    def _():
        entering[...] = inputs[...]

    cached = jnp.concatenate([c0[...], c1[...], c2[...], c3[...]], axis=0)
    conv, past = conv_block(
        entering[...], win, cached, onehot[...], masks[...], weight[...], bias[...]
    )
    conv_out[...] = conv
    for k in range(3):
        win_out[k] = past[k].astype(BF16)
    part = jnp.dot(conv.astype(BF16), proj[...], preferred_element_type=F32)

    @pl.when(step == 0)
    def _():
        acc[...] = part

    @pl.when(step > 0)
    def _():
        acc[...] += part

    @pl.when(step == STEPS - 1)
    def _():
        terms[...] = acc[...].astype(BF16)


def project_call(
    where, shares, first, gain, big, inputs, win, pieces, onehot, masks, weight, bias, proj
):
    return pl.pallas_call(
        project_kernel,
        grid_spec=pltpu.PrefetchScalarGridSpec(
            num_scalar_prefetch=1,
            grid=(STEPS,),
            in_specs=[
                *[full((ROWS, SHARE))] * 5,
                full((1, FEATURES)),
                pl.BlockSpec((CB, FEATURES), lambda j, w: (j, 0)),
                columns(ROWS),
                pl.BlockSpec((3, SLOTS, CB), lambda j, w: (0, 0, j)),
                *[columns(16, 3 * CB)] * 4,
                full((ROWS, POOL)),
                full((ROWS, LANES)),
                columns(4),
                columns(1),
                pl.BlockSpec((CB, TERMS), lambda j, w: (j, 0)),
            ],
            out_specs=[
                columns(ROWS),
                full((ROWS, TERMS)),
                pl.BlockSpec((3, SLOTS, CB), lambda j, w: (0, 0, j)),
                full((ROWS, SHARE)),
            ],
            scratch_shapes=[
                pltpu.VMEM((ROWS, TERMS), F32),
                pltpu.VMEM((4, ROWS, SHARE), BF16),
                pltpu.VMEM((ROWS, FEATURES), BF16),
                pltpu.VMEM((ROWS, CB), BF16),
            ],
        ),
        out_shape=[
            jax.ShapeDtypeStruct((ROWS, CHANNELS), F32),
            jax.ShapeDtypeStruct((ROWS, TERMS), BF16),
            jax.ShapeDtypeStruct((3, SLOTS, CHANNELS), BF16),
            jax.ShapeDtypeStruct((ROWS, SHARE), BF16),
        ],
        compiler_params=pltpu.CompilerParams(vmem_limit_bytes=40 * MIB),
        name="norm_project_conv",
    )(where, *shares, first, gain, big, inputs, win, *pieces, onehot, masks, weight, bias, proj)


def column_of(table, lane):
    index = lax.broadcasted_iota(jnp.int32, table.shape, 1)
    return jnp.sum(jnp.where(index == lane, table, 0.0), axis=1, keepdims=True)


def scan_kernel(final, *refs):
    refs = list(refs)
    take = lambda count: [refs.pop(0) for _ in range(count)]
    (where,) = take(1)
    terms = take(4)
    side_a = take(4)
    side_b = take(4)
    onehot, keep, cached_scales = take(3)
    conv, codes, scales, step_proj, step_bias, decay, skip = take(7)
    if final:
        scan_out, codes_out, scales_out = take(3)
    else:
        gate, big = take(2)
        own_out, send1, send2, send3 = take(4)
    step_low, entry, readout, fetched, natural = take(5)
    if final:
        states, scale_acc = take(2)
    else:
        acc, gated = take(2)

    step = pl.program_id(0)
    used = ROWS if final else 2 * SLOTS

    @pl.when(step == 0)
    def _():
        total = terms[0][...].astype(F32)
        for piece in terms[1:]:
            total = total + piece[...].astype(F32)
        step_low[...] = total[:, :RANK].astype(BF16)
        for n in range(STATES):
            e = jnp.broadcast_to(total[:, RANK + n : RANK + n + 1], (ROWS, LANES))
            r = jnp.broadcast_to(
                total[:, RANK + STATES + n : RANK + STATES + n + 1], (ROWS, LANES)
            )
            entry[n] = e
            readout[n] = r

    def select(side, which):
        rows = jnp.concatenate([piece[...] for piece in side], axis=0)
        fetched[...] = jnp.dot(onehot[which, :used], rows, preferred_element_type=F32)

    @pl.when(step < STEPS // 2)
    def _():
        select(side_a, 0)

    @pl.when(step >= STEPS // 2)
    def _():
        select(side_b, 1)

    sizes = softplus(
        jnp.dot(step_low[...], step_proj[...], preferred_element_type=F32) + step_bias[...]
    )
    for part in range(CB // LANES):
        cols = slice(part * LANES, (part + 1) * LANES)
        block = step * (CB // LANES) + part
        natural[...] = codes[:, :, cols].astype(F32).reshape(SLOTS * STATES, LANES)
        start_scale = jnp.broadcast_to(
            column_of(scales[...].astype(F32), block), (SLOTS, LANES)
        )
        new_scale = column_of(cached_scales[...], block)
        size = [sizes[t * SLOTS : (t + 1) * SLOTS, cols] for t in range(TICKS)]
        conv_now = [conv[t * SLOTS : (t + 1) * SLOTS, cols] for t in range(TICKS)]
        gain = [size[t] * conv_now[t] for t in range(TICKS)]
        total = [skip[:, cols] * conv_now[t] for t in range(TICKS)]
        arrived_scale = [
            jnp.broadcast_to(new_scale[t * SLOTS : (t + 1) * SLOTS], (SLOTS, LANES))
            for t in range(TICKS - 1)
        ]
        square = jnp.zeros((SLOTS, LANES), F32)
        for n in range(STATES):
            rate = decay[n : n + 1, cols] * -LOG2E
            state = natural[pl.ds(n, SLOTS, stride=STATES), :] * start_scale
            lanes = slice(n * CB + part * LANES, n * CB + (part + 1) * LANES)
            for t in range(TICKS):
                rows = slice(t * SLOTS, (t + 1) * SLOTS)
                state = jnp.exp2(size[t] * rate) * state + gain[t] * entry[n, rows]
                total[t] = total[t] + readout[n, rows] * state
                if t < TICKS - 1:
                    state = keep[rows] * state + fetched[rows, lanes] * arrived_scale[t]
            if final:
                states[n] = state
                square = square + state * state
        if not final:
            for t in range(TICKS):
                rows = slice(t * SLOTS, (t + 1) * SLOTS)
                gated[rows, cols] = (total[t] * silu(gate[rows, cols].astype(F32))).astype(BF16)
        else:
            for t in range(TICKS):
                scan_out[t * SLOTS : (t + 1) * SLOTS, cols] = total[t].astype(BF16)
            mean = jnp.sum(square, axis=1, keepdims=True) * (1.0 / (STATES * LANES))
            scale = jnp.sqrt(mean + 1e-06).astype(BF16).astype(F32)
            inverse = jnp.broadcast_to(1.0 / scale, (SLOTS, LANES))
            last = slice((TICKS - 1) * SLOTS, TICKS * SLOTS)
            kept = keep[last] > 0.5
            for n in range(STATES):
                lanes = slice(n * CB + part * LANES, n * CB + (part + 1) * LANES)
                natural[pl.ds(n, SLOTS, stride=STATES), :] = jnp.where(
                    kept, states[n] * inverse, fetched[last, lanes]
                )
            codes_out[:, :, cols] = (
                natural[...].reshape(SLOTS, STATES, LANES).astype(BF16)
            )
            chosen = jnp.where(
                kept, jnp.broadcast_to(scale, (SLOTS, LANES)), new_scale[last]
            )
            index = lax.broadcasted_iota(jnp.int32, (SLOTS, LANES), 1)
            before = jnp.where(block == 0, 0.0, scale_acc[...])
            scale_acc[...] = jnp.where(index == block, chosen, before)

    if final:

        @pl.when(step == STEPS - 1)
        def _():
            scales_out[...] = scale_acc[...].astype(BF16)

    else:
        for f in range(4):
            part = jnp.dot(
                gated[...], big[:, f * SHARE : (f + 1) * SHARE], preferred_element_type=F32
            )

            @pl.when(step == 0)
            def _():
                acc[f] = part

            @pl.when(step > 0)
            def _():
                acc[f] += part

        @pl.when(step == STEPS - 1)
        def _():
            column = where[1]
            own_out[...] = acc[column]
            send1[...] = acc[column ^ 1].astype(BF16)
            send2[...] = acc[column ^ 2].astype(BF16)
            send3[...] = acc[column ^ 3].astype(BF16)


def scan_call(
    final,
    where,
    terms,
    side_a,
    side_b,
    onehot,
    keep,
    cached_scales,
    conv,
    codes,
    scales,
    step_proj,
    step_bias,
    decay,
    skip,
    gate=None,
    big=None,
):
    half = STEPS // 2
    in_specs = [
        *[full((ROWS, TERMS))] * 4,
        *[pl.BlockSpec((16, STATES * CB), lambda j, w: (0, jnp.minimum(j, half - 1)))] * 4,
        *[pl.BlockSpec((16, STATES * CB), lambda j, w: (0, jnp.maximum(j - half, 0)))] * 4,
        full((2, ROWS, POOL)),
        full((ROWS, LANES)),
        full((ROWS, LANES)),
        columns(ROWS),
        pl.BlockSpec((SLOTS, STATES, CB), lambda j, w: (0, 0, j)),
        full((SLOTS, 16)),
        columns(RANK),
        columns(1),
        columns(STATES),
        columns(1),
    ]
    args = [*terms, *side_a, *side_b, onehot, keep, cached_scales, conv, codes, scales]
    args += [step_proj, step_bias, decay, skip]
    scratch = [
        pltpu.VMEM((ROWS, RANK), BF16),
        pltpu.VMEM((STATES, ROWS, LANES), F32),
        pltpu.VMEM((STATES, ROWS, LANES), F32),
        pltpu.VMEM((ROWS if final else 2 * SLOTS, STATES * CB), F32),
        pltpu.VMEM((SLOTS * STATES, LANES), F32),
    ]
    if final:
        out_specs = [
            columns(ROWS),
            pl.BlockSpec((SLOTS, STATES, CB), lambda j, w: (0, 0, j)),
            full((SLOTS, LANES)),
        ]
        out_shape = [
            jax.ShapeDtypeStruct((ROWS, CHANNELS), BF16),
            jax.ShapeDtypeStruct((SLOTS, STATES, CHANNELS), BF16),
            jax.ShapeDtypeStruct((SLOTS, LANES), BF16),
        ]
        scratch += [pltpu.VMEM((STATES, SLOTS, LANES), F32), pltpu.VMEM((SLOTS, LANES), F32)]
    else:
        in_specs += [columns(ROWS), pl.BlockSpec((CB, FEATURES), lambda j, w: (j, 0))]
        args += [gate, big]
        out_specs = [full((ROWS, SHARE))] * 4
        out_shape = [jax.ShapeDtypeStruct((ROWS, SHARE), F32)] + [
            jax.ShapeDtypeStruct((ROWS, SHARE), BF16)
        ] * 3
        scratch += [pltpu.VMEM((4, ROWS, SHARE), F32), pltpu.VMEM((ROWS, CB), BF16)]
    return pl.pallas_call(
        functools.partial(scan_kernel, final),
        grid_spec=pltpu.PrefetchScalarGridSpec(
            num_scalar_prefetch=1,
            grid=(STEPS,),
            in_specs=in_specs,
            out_specs=out_specs,
            scratch_shapes=scratch,
        ),
        out_shape=out_shape,
        compiler_params=pltpu.CompilerParams(vmem_limit_bytes=40 * MIB),
        name="scan_final" if final else "scan_gate_project",
    )(where, *args)


def add_kernel(where, residual, own, a, b, c, out):
    total = residual[...].astype(F32) + (
        own[...] + a[...].astype(F32) + b[...].astype(F32) + c[...].astype(F32)
    )
    out[...] = total.astype(BF16)


def add_call(where, residual, own, arrived):
    return pl.pallas_call(
        add_kernel,
        grid_spec=pltpu.PrefetchScalarGridSpec(
            num_scalar_prefetch=1,
            grid=(1,),
            in_specs=[
                pl.BlockSpec((ROWS, SHARE), lambda j, w: (0, w[1])),
                *[full((ROWS, SHARE))] * 4,
            ],
            out_specs=full((ROWS, SHARE)),
        ),
        out_shape=jax.ShapeDtypeStruct((ROWS, SHARE), BF16),
        name="add_residual",
    )(where, residual, own, *arrived)


def exchange(value, step):
    return lax.ppermute(value, "tensor", [(i, i ^ step) for i in range(4)])


def along(value, axis, step):
    if axis == "y":
        pairs = [(i, (i // 4) * 4 + (i + step) % 4) for i in range(16)]
    else:
        pairs = [(i, (i + 4 * step) % 16) for i in range(16)]
    return lax.ppermute(value, "replica", pairs)


def gather_pool(value, order):
    near = cat_rows([value] + [along(value, order[0], k) for k in (1, 2, 3)])
    return [near] + [along(near, order[1], k) for k in (1, 2, 3)]


def in_section_one(value, step):
    pairs = [(4 + i, 4 + (i ^ step)) for i in range(4)]
    return lax.ppermute(value, ("section", "tensor"), pairs)


def local(
    inner_input,
    gate_input,
    residual,
    projection,
    state_proj,
    step_proj,
    conv_weight,
    conv_bias,
    decay_rate,
    skip_gain,
    step_bias,
    norm_gain,
    state_codes,
    state_scales,
    conv_window,
    cache_codes,
    cache_scales,
    cache_window,
    finished,
    refill_source,
):
    section = lax.axis_index("section")
    column = lax.axis_index("tensor")
    replica = lax.axis_index("replica")
    where = jnp.stack([section, column]).astype(jnp.int32)

    rows = cache_window.shape[1]
    window_rows = cache_window[0].reshape(rows, 3, STEPS, CB).transpose(0, 2, 1, 3)
    small = jnp.concatenate(
        [
            window_rows.reshape(rows, 3 * CHANNELS),
            cache_scales[0],
            jnp.zeros((rows, LANES - cache_scales.shape[2]), BF16),
        ],
        axis=1,
    )
    small_pieces = gather_pool(small, "yz")
    code_rows = cache_codes[0].reshape(rows, STATES, STEPS, CB).transpose(0, 2, 1, 3)
    code_rows = code_rows.reshape(rows, STATES * CHANNELS)
    half = STATES * CHANNELS // 2
    side_a = gather_pool(code_rows[:, :half], "yz")
    side_b = gather_pool(code_rows[:, half:], "zy")

    sources = lax.dynamic_slice_in_dim(refill_source, replica * SLOTS, SLOTS, 1).reshape(ROWS)
    ended = finished.reshape(ROWS) == 1
    taken = (sources >= 0) & ended
    owner, within = sources // rows, sources % rows
    up = (replica // 4 - owner // 4) % 4
    over = (replica % 4 - owner % 4) % 4
    places = jnp.stack([(up * 4 + over) * rows + within, (over * 4 + up) * rows + within])
    onehot = (
        (places[:, :, None] == jnp.arange(POOL)[None, None, :]) & taken[None, :, None]
    ).astype(BF16)
    masks = jnp.broadcast_to(ended[:, None], (ROWS, LANES)).astype(F32)
    keep = 1.0 - masks

    window = conv_window[0].transpose(1, 0, 2)
    inputs = inner_input.reshape(ROWS, CHANNELS)
    weight = projection[0]

    conv_out, terms = conv_call(
        inputs,
        window,
        small_pieces,
        onehot[0],
        masks,
        conv_weight[0],
        conv_bias,
        state_proj[0],
    )
    tail = jnp.concatenate([piece[:, 3 * CHANNELS :] for piece in small_pieces], axis=0)
    cached_scales = jnp.dot(onehot[0], tail, preferred_element_type=F32)
    shared = (onehot, keep, cached_scales)
    layer = (step_proj[0], step_bias, decay_rate[0], skip_gain)

    all_terms = [terms] + [exchange(terms, k) for k in (1, 2, 3)]
    own, *sends = scan_call(
        False,
        where,
        all_terms,
        side_a,
        side_b,
        *shared,
        conv_out,
        state_codes[0],
        state_scales[0],
        *layer,
        gate_input.reshape(ROWS, CHANNELS),
        weight,
    )
    arrived = [exchange(value, k + 1) for k, value in enumerate(sends)]
    first = add_call(where, residual.reshape(ROWS, FEATURES), own, arrived)

    got = lax.ppermute(first, ("section", "tensor"), [(i, 4 + (i ^ 2)) for i in range(4)])
    got_a = in_section_one(got, 2)
    got_b = in_section_one(got, 1)
    got_c = in_section_one(got_a, 1)

    conv_out, terms, window_out, stream_out = project_call(
        where,
        (got, got_a, got_b, got_c),
        first,
        norm_gain[None],
        weight,
        inputs,
        window,
        small_pieces,
        onehot[0],
        masks,
        conv_weight[0],
        conv_bias,
        state_proj[0],
    )
    all_terms = [terms] + [exchange(terms, k) for k in (1, 2, 3)]
    scan_out, codes_out, scales_out = scan_call(
        True,
        where,
        all_terms,
        side_a,
        side_b,
        *shared,
        conv_out,
        state_codes[0],
        state_scales[0],
        *layer,
    )
    return (
        stream_out.reshape(TICKS, SLOTS, SHARE),
        scan_out.reshape(1, TICKS, SLOTS, CHANNELS),
        codes_out[None],
        scales_out[None, :, : state_scales.shape[2]],
        window_out.transpose(1, 0, 2)[None],
    )


def solution(mesh):
    return jax.shard_map(
        local,
        mesh=mesh,
        in_specs=(
            P(None, "replica", "tensor"),
            P(None, "replica", "tensor"),
            P(None, "replica", None),
            P("section", "tensor", None),
            P("section", "tensor", None),
            P("section", None, "tensor"),
            P("section", None, "tensor"),
            P("section", "tensor"),
            P("section", None, "tensor"),
            P("section", "tensor"),
            P("section", "tensor"),
            P(),
            P("section", "replica", None, "tensor"),
            P("section", "replica", "tensor"),
            P("section", "replica", None, "tensor"),
            P("section", "replica", None, "tensor"),
            P("section", "replica", "tensor"),
            P("section", "replica", None, "tensor"),
            P(None, "replica"),
            P(),
        ),
        out_specs=(
            P(None, "replica", "tensor"),
            P("section", None, "replica", "tensor"),
            P("section", "replica", None, "tensor"),
            P("section", "replica", "tensor"),
            P("section", "replica", None, "tensor"),
        ),
        check_vma=False,
    )
```

```python
import functools
import math

import jax
import jax.numpy as jnp
from jax import lax
from jax.experimental import pallas as pl
from jax.experimental.pallas import tpu as pltpu
from jax.sharding import PartitionSpec as P

RANK = 256
STATES = 16
TICKS = 3
SLOTS = 32
ROWS = TICKS * SLOTS
CHANNELS = 2048
FEATURES = 4096
SHARE = FEATURES // 4
CB = 512
STEPS = CHANNELS // CB
LANES = 128
TERMS = RANK + 2 * STATES
POOL = 64
WIDE = 4 * CB
CODE_LANES = STATES * CB
GROUP = CODE_LANES + WIDE
LOG2E = math.log2(math.e)
F32 = jnp.float32
BF16 = jnp.bfloat16
MIB = 1024 * 1024
COST = pl.CostEstimate(flops=1, transcendentals=0, bytes_accessed=1)


def cat_kernel(a, b, c, d, first, last):
    for block, out in enumerate((first, last)):
        cols = slice(block * GROUP, (block + 1) * GROUP)
        out[...] = jnp.concatenate([a[:, cols], b[:, cols], c[:, cols], d[:, cols]], axis=0)


def cat_rows(pieces):
    shape = jax.ShapeDtypeStruct((16, GROUP), BF16)
    return pl.pallas_call(
        cat_kernel,
        out_shape=[shape, shape],
        compiler_params=pltpu.CompilerParams(vmem_limit_bytes=48 * MIB),
        cost_estimate=COST,
        name="cat_rows",
    )(*pieces)


HELD = pl.BlockSpec(memory_space=pltpu.VMEM)
SCALARS = pl.BlockSpec(memory_space=pltpu.SMEM)
ANYWHERE = pl.BlockSpec(memory_space=pltpu.HBM)


def held(shape, dtype):
    return pltpu.VMEM(shape, dtype)


def call(kernel, name, mebibytes, in_specs, out_shape, scratch, args):
    return pl.pallas_call(
        kernel,
        in_specs=in_specs,
        out_specs=[HELD] * len(out_shape) if isinstance(out_shape, list) else HELD,
        out_shape=out_shape,
        scratch_shapes=scratch,
        compiler_params=pltpu.CompilerParams(vmem_limit_bytes=mebibytes * MIB),
        cost_estimate=COST,
        name=name,
    )(*args)


def silu(x):
    return x / (1.0 + jnp.exp(-x))


def softplus(x):
    return jnp.maximum(x, 0.0) + jnp.log1p(jnp.exp(-jnp.abs(x)))


def column_of(table, lane):
    index = lax.broadcasted_iota(jnp.int32, table.shape, 1)
    return jnp.sum(jnp.where(index == lane, table, 0.0), axis=1, keepdims=True)


def tile(index):
    return pl.ds(pl.multiple_of(index * LANES, LANES), LANES)


def fill_kernel(*refs):
    sources, target, arrived = refs[:-2], refs[-2], refs[-1]
    copies, row = [], 0
    for i, source in enumerate(sources):
        count = source.shape[0]
        copies.append(
            pltpu.make_async_copy(source, target.at[pl.ds(row, count)], arrived.at[i])
        )
        copies[-1].start()
        row += count
    for copy in copies:
        copy.wait()


def fill_call(name, arrays):
    rows = sum(array.shape[0] for array in arrays)
    return call(
        fill_kernel,
        name,
        14,
        [ANYWHERE] * len(arrays),
        held((rows, arrays[0].shape[1]), BF16),
        [pltpu.SemaphoreType.DMA((len(arrays),))],
        arrays,
    )


def unfold_kernel(codes, scales, states, natural):
    def unfold(block, carry):
        cols = tile(block)
        natural[...] = codes[:, :, cols].astype(F32).reshape(SLOTS * STATES, LANES)
        scale = jnp.broadcast_to(column_of(scales[...].astype(F32), block), (SLOTS, LANES))
        for n in range(STATES):
            states[n, :, cols] = natural[pl.ds(n, SLOTS, stride=STATES), :] * scale
        return carry

    lax.fori_loop(0, CHANNELS // LANES, unfold, 0)


def unfold_call(codes, scales):
    return call(
        unfold_kernel,
        "unfold_states",
        14,
        [HELD] * 2,
        held((STATES, SLOTS, CHANNELS), F32),
        [pltpu.VMEM((SLOTS * STATES, LANES), F32)],
        [codes, scales],
    )


def pool_kernel(*refs):
    pieces, pool, arrived = refs[: 4 * STEPS], refs[-2], refs[-1]
    copies = [
        pltpu.make_async_copy(piece, pool.at[i // 4, pl.ds(i % 4 * 16, 16)], arrived.at[i])
        for i, piece in enumerate(pieces)
    ]
    for copy in copies:
        copy.start()
    for copy in copies:
        copy.wait()


def pool_call(pieces):
    return call(
        pool_kernel,
        "pool_rows",
        14,
        [ANYWHERE] * (4 * STEPS),
        held((STEPS, POOL, GROUP), BF16),
        [pltpu.SemaphoreType.DMA((4 * STEPS,))],
        pieces,
    )


STEP_ROWS, INPUT_ROWS, GATE_ROWS, WINDOW_ROWS = 0, RANK, RANK + ROWS, RANK + 2 * ROWS
TAP_ROW, BIAS_ROW, DECAY_ROW, SKIP_ROW, OFFSET_ROW = 0, 4, 5, 21, 22


def conv_block(inputs, store, fetched, keep, gains, cols):
    past = [
        store[WINDOW_ROWS + k * SLOTS : WINDOW_ROWS + (k + 1) * SLOTS, cols].astype(F32)
        for k in range(3)
    ]
    outs = []
    for tick in range(TICKS):
        rows = slice(tick * SLOTS, (tick + 1) * SLOTS)
        taps = past + [inputs[rows].astype(F32)]
        total = gains[BIAS_ROW : BIAS_ROW + 1, cols]
        for k in range(4):
            total = total + gains[TAP_ROW + k : TAP_ROW + k + 1, cols] * taps[k]
        outs.append(silu(total))
        stays = keep[rows, :1] > 0.5
        past = [
            jnp.where(stays, taps[k + 1], fetched[rows, k * CB : (k + 1) * CB]) for k in range(3)
        ]
    return jnp.concatenate(outs, axis=0), past


def conv_kernel(store, onehot, keep, gains, proj, pool, conv_out, terms, scales):
    total = jnp.zeros((ROWS, TERMS), F32)
    for block in range(STEPS):
        cols = slice(block * CB, (block + 1) * CB)
        fetched = jnp.dot(
            onehot[block // 2], pool[block, :, CODE_LANES:], preferred_element_type=F32
        )
        if block == 0:
            scales[...] = fetched[:, 3 * CB : 3 * CB + LANES]
        inputs = store[INPUT_ROWS : INPUT_ROWS + ROWS, cols]
        conv, _ = conv_block(inputs, store, fetched, keep, gains, cols)
        conv_out[:, cols] = conv
        total = total + jnp.dot(conv.astype(BF16), proj[cols], preferred_element_type=F32)
    terms[...] = total.astype(BF16)


def conv_call(args):
    return call(
        conv_kernel,
        "conv_terms",
        14,
        [HELD] * len(args),
        [
            jax.ShapeDtypeStruct((ROWS, CHANNELS), F32),
            jax.ShapeDtypeStruct((ROWS, TERMS), BF16),
            jax.ShapeDtypeStruct((ROWS, LANES), F32),
        ],
        [],
        args,
    )


def project_kernel(
    where,
    s_own,
    s_a,
    s_b,
    s_c,
    first,
    gain,
    store,
    onehot,
    keep,
    gains,
    proj,
    pool,
    big,
    conv_out,
    terms,
    win_out,
    stream_out,
    values,
    normed,
    entering,
    weight,
    loaded,
):
    section, column = where[0], where[1]
    parts = [
        pltpu.make_async_copy(big.at[pl.ds(b * CB, CB)], weight.at[b], loaded.at[b])
        for b in range(STEPS)
    ]
    for part in parts:
        part.start()

    @pl.when(section == 0)
    def _():
        stream_out[...] = first[...]
        entering[...] = store[INPUT_ROWS : INPUT_ROWS + ROWS]

    @pl.when(section == 1)
    def _():
        values[column ^ 2] = s_own[...]
        values[column] = s_a[...]
        values[column ^ 3] = s_b[...]
        values[column ^ 1] = s_c[...]
        stream_out[...] = s_a[...]
        total = jnp.zeros((ROWS, 1), F32)
        for f in range(4):
            v = values[f].astype(F32)
            total = total + jnp.sum(v * v, axis=1, keepdims=True)
        factor = lax.rsqrt(total * (1.0 / FEATURES) + 1e-05)
        for f in range(4):
            cols = slice(f * SHARE, (f + 1) * SHARE)
            v = values[f].astype(F32)
            normed[:, cols] = (v * factor * gain[:, cols].astype(F32)).astype(BF16)

    total = jnp.zeros((ROWS, TERMS), F32)
    for block in range(STEPS):
        cols = slice(block * CB, (block + 1) * CB)
        parts[block].wait()

        @pl.when(section == 1)
        def _():
            entering[:, cols] = lax.dot_general(
                normed[...], weight[block], (((1,), (1,)), ((), ())), preferred_element_type=F32
            ).astype(BF16)

        fetched = jnp.dot(
            onehot[block // 2], pool[block, :, CODE_LANES:], preferred_element_type=F32
        )
        conv, past = conv_block(entering[:, cols], store, fetched, keep, gains, cols)
        conv_out[:, cols] = conv
        for k in range(3):
            win_out[k, :, cols] = past[k].astype(BF16)
        total = total + jnp.dot(conv.astype(BF16), proj[cols], preferred_element_type=F32)
    terms[...] = total.astype(BF16)


def project_call(where, shares, args):
    return call(
        project_kernel,
        "norm_project_conv",
        36,
        [SCALARS] + [HELD] * (3 + len(args)) + [ANYWHERE],
        [
            jax.ShapeDtypeStruct((ROWS, CHANNELS), F32),
            jax.ShapeDtypeStruct((ROWS, TERMS), BF16),
            jax.ShapeDtypeStruct((3, SLOTS, CHANNELS), BF16),
            jax.ShapeDtypeStruct((ROWS, SHARE), BF16),
        ],
        [
            pltpu.VMEM((4, ROWS, SHARE), BF16),
            pltpu.VMEM((ROWS, FEATURES), BF16),
            pltpu.VMEM((ROWS, CHANNELS), BF16),
            pltpu.VMEM((STEPS, CB, FEATURES), BF16),
            pltpu.SemaphoreType.DMA((STEPS,)),
        ],
        [where, *shares, *args],
    )


def scan_kernel(final, *refs):
    refs = list(refs)
    take = lambda count: [refs.pop(0) for _ in range(count)]
    (where,) = take(1)
    terms = take(4)
    onehot, keep, cached_scales, pool, conv, start, store, gains = take(8)
    if final:
        scan_out, codes_out, scales_out = take(3)
    else:
        (big,) = take(1)
        sends = take(4)
    entry, readout, fetched, sizes = take(4)
    if final:
        states, natural, scale_acc = take(3)
    else:
        gated, weight, loaded = take(3)
        parts = [
            pltpu.make_async_copy(
                big.at[pl.ds(b * CB, CB)], weight.at[pl.ds(b * CB, CB)], loaded.at[b]
            )
            for b in range(STEPS)
        ]
        for copy in parts:
            copy.start()
    used = ROWS if final else 2 * SLOTS

    def gate(t, cols):
        first = GATE_ROWS + t * SLOTS
        return store[first : first + SLOTS, cols].astype(F32)

    total = terms[0][...].astype(F32)
    for piece in terms[1:]:
        total = total + piece[...].astype(F32)
    sizes[...] = softplus(
        jnp.dot(
            total[:, :RANK].astype(BF16),
            store[STEP_ROWS : STEP_ROWS + RANK],
            preferred_element_type=F32,
        )
        + gains[OFFSET_ROW : OFFSET_ROW + 1]
    )
    for n in range(STATES):
        e, r = RANK + n, RANK + STATES + n
        entry[n] = jnp.broadcast_to(total[:, e : e + 1], (ROWS, LANES))
        readout[n] = jnp.broadcast_to(total[:, r : r + 1], (ROWS, LANES))
    if final:
        scale_acc[...] = jnp.zeros_like(scale_acc)

    def scan_block(block, carry):
        fetched[...] = jnp.dot(
            onehot[block // 2, :used],
            pool[block, :, :CODE_LANES],
            preferred_element_type=F32,
        )
        for part in range(CB // LANES):
            index = block * (CB // LANES) + part
            scan_tile(index, part)
        return carry

    def scan_tile(index, part):
        cols = tile(index)
        new_scale = column_of(cached_scales[...], index)
        size = [sizes[t * SLOTS : (t + 1) * SLOTS, cols] for t in range(TICKS)]
        conv_now = [conv[t * SLOTS : (t + 1) * SLOTS, cols] for t in range(TICKS)]
        gain = [size[t] * conv_now[t] for t in range(TICKS)]
        total = [gains[SKIP_ROW : SKIP_ROW + 1, cols] * conv_now[t] for t in range(TICKS)]
        arrived_scale = [
            jnp.broadcast_to(new_scale[t * SLOTS : (t + 1) * SLOTS], (SLOTS, LANES))
            for t in range(TICKS - 1)
        ]
        square = jnp.zeros((SLOTS, LANES), F32)
        for n in range(STATES):
            rate = gains[DECAY_ROW + n : DECAY_ROW + n + 1, cols] * -LOG2E
            state = start[n, :, cols]
            lanes = slice(n * CB + part * LANES, n * CB + (part + 1) * LANES)
            for t in range(TICKS):
                rows = slice(t * SLOTS, (t + 1) * SLOTS)
                state = jnp.exp2(size[t] * rate) * state + gain[t] * entry[n, rows]
                total[t] = total[t] + readout[n, rows] * state
                if t < TICKS - 1:
                    state = keep[rows] * state + fetched[rows, lanes] * arrived_scale[t]
            if final:
                states[n] = state
                square = square + state * state
        if not final:
            for t in range(TICKS):
                rows = slice(t * SLOTS, (t + 1) * SLOTS)
                gated[rows, cols] = (total[t] * silu(gate(t, cols))).astype(BF16)
            return
        for t in range(TICKS):
            scan_out[t * SLOTS : (t + 1) * SLOTS, cols] = total[t].astype(BF16)
        mean = jnp.sum(square, axis=1, keepdims=True) * (1.0 / (STATES * LANES))
        scale = jnp.sqrt(mean + 1e-06).astype(BF16).astype(F32)
        inverse = jnp.broadcast_to(1.0 / scale, (SLOTS, LANES))
        last = slice((TICKS - 1) * SLOTS, TICKS * SLOTS)
        kept = keep[last] > 0.5
        for n in range(STATES):
            lanes = slice(n * CB + part * LANES, n * CB + (part + 1) * LANES)
            natural[pl.ds(n, SLOTS, stride=STATES), :] = jnp.where(
                kept, states[n] * inverse, fetched[last, lanes]
            )
        codes_out[:, :, cols] = natural[...].reshape(SLOTS, STATES, LANES).astype(BF16)
        chosen = jnp.where(kept, jnp.broadcast_to(scale, (SLOTS, LANES)), new_scale[last])
        lane = lax.broadcasted_iota(jnp.int32, (SLOTS, LANES), 1)
        scale_acc[...] = jnp.where(lane == index, chosen, scale_acc[...])

    lax.fori_loop(0, STEPS, scan_block, 0)
    if final:
        scales_out[...] = scale_acc[...].astype(BF16)
        return
    for copy in parts:
        copy.wait()
    column = where[1]
    for k, out in enumerate(sends):
        cols = pl.ds(pl.multiple_of((column ^ k) * SHARE, SHARE), SHARE)
        out[...] = jnp.dot(gated[...], weight[:, cols], preferred_element_type=F32).astype(out.dtype)


def scan_call(final, where, terms, args):
    scratch = [
        pltpu.VMEM((STATES, ROWS, LANES), F32),
        pltpu.VMEM((STATES, ROWS, LANES), F32),
        pltpu.VMEM((ROWS if final else 2 * SLOTS, STATES * CB), F32),
        pltpu.VMEM((ROWS, CHANNELS), F32),
    ]
    if final:
        out_shape = [
            jax.ShapeDtypeStruct((ROWS, CHANNELS), BF16),
            jax.ShapeDtypeStruct((SLOTS, STATES, CHANNELS), BF16),
            jax.ShapeDtypeStruct((SLOTS, LANES), BF16),
        ]
        scratch += [
            pltpu.VMEM((STATES, SLOTS, LANES), F32),
            pltpu.VMEM((SLOTS * STATES, LANES), F32),
            pltpu.VMEM((SLOTS, LANES), F32),
        ]
    else:
        out_shape = [jax.ShapeDtypeStruct((ROWS, SHARE), F32)] + [
            jax.ShapeDtypeStruct((ROWS, SHARE), BF16)
        ] * 3
        scratch += [
            pltpu.VMEM((ROWS, CHANNELS), BF16),
            pltpu.VMEM((CHANNELS, FEATURES), BF16),
            pltpu.SemaphoreType.DMA((STEPS,)),
        ]
    return call(
        functools.partial(scan_kernel, final),
        "scan_final" if final else "scan_gate_project",
        16 if final else 36,
        [SCALARS] + [HELD] * (4 + len(args) - (not final)) + [ANYWHERE] * (not final),
        out_shape,
        scratch,
        [where, *terms, *args],
    )


def add_kernel(residual, own, a, b, c, out):
    total = residual[...].astype(F32) + (
        own[...] + a[...].astype(F32) + b[...].astype(F32) + c[...].astype(F32)
    )
    out[...] = total.astype(BF16)


def add_call(args):
    return call(
        add_kernel,
        "add_residual",
        14,
        [HELD] * 5,
        [jax.ShapeDtypeStruct((ROWS, SHARE), BF16)],
        [],
        args,
    )[0]


def exchange(value, step):
    return lax.ppermute(value, "tensor", [(i, i ^ step) for i in range(4)])


def along(value, axis, step):
    if axis == "y":
        pairs = [(i, (i // 4) * 4 + (i + step) % 4) for i in range(16)]
    else:
        pairs = [(i, (i + 4 * step) % 16) for i in range(16)]
    return lax.ppermute(value, "replica", pairs)


def gather_pool(value, near, far):
    first, last = cat_rows([value] + [along(value, near, k) for k in (1, 2, 3)])
    first_below, last_above = along(first, far, 1), along(last, far, 3)
    last_below, first_above = along(last, far, 1), along(first, far, 3)
    first_far, last_far = along(first_below, far, 1), along(last_above, far, 3)
    return [first, first_below, first_far, first_above, last, last_below, last_far, last_above]


def in_section_one(value, step):
    pairs = [(4 + i, 4 + (i ^ step)) for i in range(4)]
    return lax.ppermute(value, ("section", "tensor"), pairs)


def local(
    inner_input,
    gate_input,
    residual,
    projection,
    state_proj,
    step_proj,
    conv_weight,
    conv_bias,
    decay_rate,
    skip_gain,
    step_bias,
    norm_gain,
    state_codes,
    state_scales,
    conv_window,
    cache_codes,
    cache_scales,
    cache_window,
    finished,
    refill_source,
):
    section = lax.axis_index("section")
    column = lax.axis_index("tensor")
    replica = lax.axis_index("replica")
    where = jnp.stack([section, column]).astype(jnp.int32)

    rows = cache_window.shape[1]
    blocks = STEPS // 2
    codes = cache_codes[0].reshape(rows, STATES, 2, blocks, CB).transpose(2, 0, 3, 1, 4)
    windows = cache_window[0].reshape(rows, 3, 2, blocks, CB).transpose(2, 0, 3, 1, 4)
    room = CB - cache_scales.shape[2]
    tail = jnp.pad(cache_scales[0], ((0, 0), (0, room)))[None, :, None]
    cached = jnp.concatenate(
        [
            codes.reshape(2, rows, blocks, CODE_LANES),
            windows.reshape(2, rows, blocks, 3 * CB),
            jnp.broadcast_to(tail, (2, rows, blocks, CB)),
        ],
        axis=3,
    ).reshape(2, rows, blocks * GROUP)
    pieces = gather_pool(cached[0], "y", "z") + gather_pool(cached[1], "z", "y")

    sources = lax.dynamic_slice_in_dim(refill_source, replica * SLOTS, SLOTS, 1).reshape(ROWS)
    ended = finished.reshape(ROWS) == 1
    taken = (sources >= 0) & ended
    owner, within = sources // rows, sources % rows
    up = (replica // 4 - owner // 4) % 4
    over = (replica % 4 - owner % 4) % 4
    places = jnp.stack([(up * 4 + over) * rows + within, (over * 4 + up) * rows + within])
    onehot = (
        (places[:, :, None] == jnp.arange(POOL)[None, None, :]) & taken[None, :, None]
    ).astype(BF16)
    keep = jnp.broadcast_to(~ended[:, None], (ROWS, LANES)).astype(F32)

    gains = jnp.concatenate(
        [conv_weight[0], conv_bias, decay_rate[0], skip_gain, step_bias], axis=0
    )

    small = (onehot, keep, gains, where, residual.reshape(ROWS, FEATURES))
    flat = (
        step_proj[0],
        inner_input.reshape(ROWS, CHANNELS),
        gate_input.reshape(ROWS, CHANNELS),
        conv_window[0].transpose(1, 0, 2).reshape(ROWS, CHANNELS),
    )
    small, flat, codes, weight, pieces[0] = lax.optimization_barrier(
        (small, flat, state_codes[0], projection[0], pieces[0])
    )
    onehot, keep, gains, where, residual_rows = small
    store = fill_call("hold_store", list(flat))
    states = unfold_call(codes, state_scales[0])
    column_share = lax.dynamic_slice_in_dim(residual_rows, column * SHARE, SHARE, 1)
    pool = pool_call(pieces)

    conv_args = (store, onehot, keep, gains, state_proj[0], pool)
    conv_out, terms, cached_scales = conv_call(conv_args)
    all_terms = [terms] + [exchange(terms, k) for k in (1, 2, 3)]
    shared = (onehot, keep, cached_scales, pool)
    layer = (states, store, gains)
    own, *sends = scan_call(False, where, all_terms, (*shared, conv_out, *layer, weight))
    arrived = [exchange(value, k + 1) for k, value in enumerate(sends)]
    first = add_call((column_share, own, *arrived))

    got = lax.ppermute(first, ("section", "tensor"), [(i, 4 + (i ^ 2)) for i in range(4)])
    got_a = in_section_one(got, 2)
    got_b = in_section_one(got, 1)
    got_c = in_section_one(got_a, 1)

    conv_out, terms, window_out, stream_out = project_call(
        where, (got, got_a, got_b, got_c), (first, norm_gain[None], *conv_args, weight)
    )
    all_terms = [terms] + [exchange(terms, k) for k in (1, 2, 3)]
    scan_out, codes_out, scales_out = scan_call(
        True, where, all_terms, (*shared, conv_out, *layer)
    )
    return (
        stream_out.reshape(TICKS, SLOTS, SHARE),
        scan_out.reshape(1, TICKS, SLOTS, CHANNELS),
        codes_out[None],
        scales_out[None, :, : state_scales.shape[2]],
        window_out.transpose(1, 0, 2)[None],
    )


def solution(mesh):
    return jax.shard_map(
        local,
        mesh=mesh,
        in_specs=(
            P(None, "replica", "tensor"),
            P(None, "replica", "tensor"),
            P(None, "replica", None),
            P("section", "tensor", None),
            P("section", "tensor", None),
            P("section", None, "tensor"),
            P("section", None, "tensor"),
            P("section", "tensor"),
            P("section", None, "tensor"),
            P("section", "tensor"),
            P("section", "tensor"),
            P(),
            P("section", "replica", None, "tensor"),
            P("section", "replica", "tensor"),
            P("section", "replica", None, "tensor"),
            P("section", "replica", None, "tensor"),
            P("section", "replica", "tensor"),
            P("section", "replica", None, "tensor"),
            P(None, "replica"),
            P(),
        ),
        out_specs=(
            P(None, "replica", "tensor"),
            P("section", None, "replica", "tensor"),
            P("section", "replica", None, "tensor"),
            P("section", "replica", "tensor"),
            P("section", "replica", None, "tensor"),
        ),
        check_vma=False,
    )
```

```python
import functools
import math

import jax
import jax.numpy as jnp
from jax import lax
from jax.experimental import pallas as pl
from jax.experimental.pallas import tpu as pltpu
from jax.sharding import PartitionSpec as P

RANK = 256
STATES = 16
TICKS = 3
SLOTS = 32
ROWS = TICKS * SLOTS
CHANNELS = 2048
FEATURES = 4096
SHARE = FEATURES // 4
CB = 512
STEPS = CHANNELS // CB
LANES = 128
TERMS = RANK + 2 * STATES
POOL = 64
WIDE = 4 * CB
CODE_LANES = STATES * CB
GROUP = CODE_LANES + WIDE
LOG2E = math.log2(math.e)
F32 = jnp.float32
BF16 = jnp.bfloat16
MIB = 1024 * 1024
COST = pl.CostEstimate(flops=1, transcendentals=0, bytes_accessed=1)


HELD = pl.BlockSpec(memory_space=pltpu.VMEM)
SCALARS = pl.BlockSpec(memory_space=pltpu.SMEM)
ANYWHERE = pl.BlockSpec(memory_space=pltpu.HBM)


def held(shape, dtype):
    return pltpu.VMEM(shape, dtype)


def call(kernel, name, mebibytes, in_specs, out_shape, scratch, args, out_specs=None):
    if out_specs is None:
        out_specs = [HELD] * len(out_shape) if isinstance(out_shape, list) else HELD
    return pl.pallas_call(
        kernel,
        in_specs=in_specs,
        out_specs=out_specs,
        out_shape=out_shape,
        scratch_shapes=scratch,
        compiler_params=pltpu.CompilerParams(vmem_limit_bytes=mebibytes * MIB),
        cost_estimate=COST,
        name=name,
    )(*args)


def cat_kernel(a, b, c, d, first, last, held, left):
    copies = []
    for block, out in enumerate((first, last)):
        cols = slice(block * GROUP, (block + 1) * GROUP)
        held[block] = jnp.concatenate(
            [a[:, cols], b[:, cols], c[:, cols], d[:, cols]], axis=0
        )
        copies.append(pltpu.make_async_copy(held.at[block], out, left.at[block]))
        copies[-1].start()
    for copy in copies:
        copy.wait()


def cat_rows(pieces):
    shape = jax.ShapeDtypeStruct((16, GROUP), BF16)
    return call(
        cat_kernel,
        "cat_rows",
        48,
        [HELD] * 4,
        [shape, shape],
        [pltpu.VMEM((2, 16, GROUP), BF16), pltpu.SemaphoreType.DMA((2,))],
        pieces,
        [ANYWHERE] * 2,
    )


def silu(x):
    return x / (1.0 + jnp.exp(-x))


def softplus(x):
    return jnp.maximum(x, 0.0) + jnp.log1p(jnp.exp(-jnp.abs(x)))


def column_of(table, lane):
    index = lax.broadcasted_iota(jnp.int32, table.shape, 1)
    return jnp.sum(jnp.where(index == lane, table, 0.0), axis=1, keepdims=True)


def tile(index):
    return pl.ds(pl.multiple_of(index * LANES, LANES), LANES)


def fill_kernel(*refs):
    sources, target, arrived = refs[:-2], refs[-2], refs[-1]
    copies, row = [], 0
    for i, source in enumerate(sources):
        count = source.shape[0]
        copies.append(
            pltpu.make_async_copy(source, target.at[pl.ds(row, count)], arrived.at[i])
        )
        copies[-1].start()
        row += count
    for copy in copies:
        copy.wait()


def fill_call(name, arrays):
    rows = sum(array.shape[0] for array in arrays)
    return call(
        fill_kernel,
        name,
        14,
        [ANYWHERE] * len(arrays),
        held((rows, arrays[0].shape[1]), BF16),
        [pltpu.SemaphoreType.DMA((len(arrays),))],
        arrays,
    )


def arrange_kernel(codes, windows, scales, first, last, code_rows, window_rows):
    rows = codes.shape[0]
    for part in range(CHANNELS // LANES):
        code_rows[part] = (
            codes[:, :, part * LANES : (part + 1) * LANES]
            .astype(F32)
            .reshape(rows * STATES, LANES)
        )
    for k in range(3):
        window_rows[k * 8 : k * 8 + rows] = windows[k].astype(F32)
    for block in range(STEPS):
        out = (first, last)[block // 2]
        base = block % 2 * GROUP
        cols = slice(block * CB, (block + 1) * CB)
        for n in range(STATES):
            for part in range(CB // LANES):
                lanes = slice(base + n * CB + part * LANES, base + n * CB + (part + 1) * LANES)
                out[:, lanes] = code_rows[
                    block * (CB // LANES) + part, pl.ds(n, rows, stride=STATES), :
                ].astype(BF16)
        base += CODE_LANES
        for k in range(3):
            out[:, base + k * CB : base + (k + 1) * CB] = window_rows[
                k * 8 : k * 8 + rows, cols
            ].astype(BF16)
        out[:, base + 3 * CB : base + 4 * CB] = jnp.zeros((rows, CB), BF16)
        out[:, base + 3 * CB : base + 3 * CB + scales.shape[1]] = scales[...]


def arrange_call(codes, windows, scales):
    rows = codes.shape[0]
    half = jax.ShapeDtypeStruct((rows, STEPS // 2 * GROUP), BF16)
    return call(
        arrange_kernel,
        "arrange_rows",
        60,
        [HELD] * 3,
        [half, half],
        [
            pltpu.VMEM((CHANNELS // LANES, rows * STATES, LANES), F32),
            pltpu.VMEM((24, CHANNELS), F32),
        ],
        [codes, windows, scales],
    )


def plan_kernel(where, sources, ended, onehot, keep):
    source, over = sources[...], ended[...]
    owner, within = source >> 2, source & 3
    z = (where[2] - (owner >> 2)) & 3
    y = (where[3] - (owner & 3)) & 3
    taken = (source >= 0) & (over == 1)
    row = lax.broadcasted_iota(jnp.int32, (POOL, LANES), 0)
    for half, place in enumerate((z * 16 + y * 4 + within, y * 16 + z * 4 + within)):
        place = jnp.where(taken, place, -1)
        chosen = jnp.where(row == place, 1.0, 0.0).astype(F32)
        onehot[half] = chosen.T[:ROWS].astype(BF16)
    stays = jnp.where(over == 1, 0.0, 1.0).astype(F32)
    keep[...] = jnp.broadcast_to(stays, (LANES, LANES)).T[:ROWS]


def plan_call(where, sources, ended):
    return call(
        plan_kernel,
        "plan_rows",
        14,
        [SCALARS, HELD, HELD],
        [
            jax.ShapeDtypeStruct((2, ROWS, POOL), BF16),
            jax.ShapeDtypeStruct((ROWS, LANES), F32),
        ],
        [],
        [where, sources, ended],
    )


def unfold_kernel(codes, scales, states, natural):
    def unfold(block, carry):
        cols = tile(block)
        natural[...] = codes[:, :, cols].astype(F32).reshape(SLOTS * STATES, LANES)
        scale = jnp.broadcast_to(column_of(scales[...].astype(F32), block), (SLOTS, LANES))
        for n in range(STATES):
            states[n, :, cols] = natural[pl.ds(n, SLOTS, stride=STATES), :] * scale
        return carry

    lax.fori_loop(0, CHANNELS // LANES, unfold, 0)


def unfold_call(codes, scales):
    return call(
        unfold_kernel,
        "unfold_states",
        14,
        [HELD] * 2,
        held((STATES, SLOTS, CHANNELS), F32),
        [pltpu.VMEM((SLOTS * STATES, LANES), F32)],
        [codes, scales],
    )


def pool_kernel(*refs):
    pieces, pool, arrived = refs[: 4 * STEPS], refs[-2], refs[-1]
    copies = [
        pltpu.make_async_copy(piece, pool.at[i // 4, pl.ds(i % 4 * 16, 16)], arrived.at[i])
        for i, piece in enumerate(pieces)
    ]
    for copy in copies:
        copy.start()
    for copy in copies:
        copy.wait()


def pool_call(pieces):
    return call(
        pool_kernel,
        "pool_rows",
        50,
        [ANYWHERE] * (4 * STEPS),
        held((STEPS, POOL, GROUP), BF16),
        [pltpu.SemaphoreType.DMA((4 * STEPS,))],
        pieces,
    )


STEP_ROWS, INPUT_ROWS, GATE_ROWS, WINDOW_ROWS = 0, RANK, RANK + ROWS, RANK + 2 * ROWS
TAP_ROW, BIAS_ROW, DECAY_ROW, SKIP_ROW, OFFSET_ROW = 0, 4, 5, 21, 22


def conv_block(inputs, store, fetched, keep, gains, cols):
    past = [
        store[WINDOW_ROWS + k * SLOTS : WINDOW_ROWS + (k + 1) * SLOTS, cols].astype(F32)
        for k in range(3)
    ]
    outs = []
    for tick in range(TICKS):
        rows = slice(tick * SLOTS, (tick + 1) * SLOTS)
        taps = past + [inputs[rows].astype(F32)]
        total = gains[BIAS_ROW : BIAS_ROW + 1, cols]
        for k in range(4):
            total = total + gains[TAP_ROW + k : TAP_ROW + k + 1, cols] * taps[k]
        outs.append(silu(total))
        stays = keep[rows, :1] > 0.5
        past = [jnp.where(stays, taps[k + 1], fetched(k, rows)) for k in range(3)]
    return jnp.concatenate(outs, axis=0), past


def conv_kernel(
    store, onehot, keep, gains, proj, pool, conv_out, terms, scales, taken_out, taken, left
):
    copies = []
    total = jnp.zeros((ROWS, TERMS), F32)
    for block in range(STEPS):
        cols = slice(block * CB, (block + 1) * CB)
        fetched = jnp.dot(
            onehot[block // 2], pool[block, :, CODE_LANES:], preferred_element_type=F32
        )
        if block == 0:
            scales[...] = fetched[:, 3 * CB : 3 * CB + LANES]
        for k in range(3):
            taken[block, k] = fetched[:, k * CB : (k + 1) * CB].astype(BF16)
        copies.append(
            pltpu.make_async_copy(taken.at[block], taken_out.at[block], left.at[block])
        )
        copies[-1].start()
        inputs = store[INPUT_ROWS : INPUT_ROWS + ROWS, cols]
        conv, _ = conv_block(
            inputs, store, lambda k, rows: fetched[rows, k * CB : (k + 1) * CB], keep, gains, cols
        )
        conv_out[:, cols] = conv
        total = total + lax.dot_general(
            conv.astype(BF16), proj[:, cols], (((1,), (1,)), ((), ())), preferred_element_type=F32
        )
    terms[...] = total.astype(BF16)
    for copy in copies:
        copy.wait()


def conv_call(args):
    return call(
        conv_kernel,
        "conv_terms",
        14,
        [HELD] * len(args),
        [
            jax.ShapeDtypeStruct((ROWS, CHANNELS), F32),
            jax.ShapeDtypeStruct((ROWS, TERMS), BF16),
            jax.ShapeDtypeStruct((ROWS, LANES), F32),
            jax.ShapeDtypeStruct((STEPS, 3, ROWS, CB), BF16),
        ],
        [pltpu.VMEM((STEPS, 3, ROWS, CB), BF16), pltpu.SemaphoreType.DMA((STEPS,))],
        args,
        [HELD] * 3 + [ANYWHERE],
    )


def project_kernel(
    where,
    s_own,
    s_a,
    s_b,
    s_c,
    gain,
    store,
    keep,
    gains,
    proj,
    taken,
    big,
    conv_out,
    terms,
    win_out,
    values,
    normed,
    entering,
):
    section, column = where[0], where[1]

    @pl.when(section == 0)
    def _():
        entering[...] = store[INPUT_ROWS : INPUT_ROWS + ROWS]

    @pl.when(section == 1)
    def _():
        values[column] = s_own[...]
        values[column ^ 2] = s_a[...]
        values[column ^ 1] = s_b[...]
        values[column ^ 3] = s_c[...]
        total = jnp.zeros((ROWS, 1), F32)
        for f in range(4):
            v = values[f].astype(F32)
            total = total + jnp.sum(v * v, axis=1, keepdims=True)
        factor = lax.rsqrt(total * (1.0 / FEATURES) + 1e-05)
        for f in range(4):
            cols = slice(f * SHARE, (f + 1) * SHARE)
            v = values[f].astype(F32)
            normed[:, cols] = (v * factor * gain[:, cols].astype(F32)).astype(BF16)

    total = jnp.zeros((ROWS, TERMS), F32)
    for block in range(STEPS):
        cols = slice(block * CB, (block + 1) * CB)

        @pl.when(section == 1)
        def _():
            entering[:, cols] = lax.dot_general(
                normed[...], big[cols], (((1,), (1,)), ((), ())), preferred_element_type=F32
            ).astype(BF16)

        conv, past = conv_block(
            entering[:, cols],
            store,
            lambda k, rows: taken[block, k, rows].astype(F32),
            keep,
            gains,
            cols,
        )
        conv_out[:, cols] = conv
        for k in range(3):
            win_out[k, :, cols] = past[k].astype(BF16)
        total = total + lax.dot_general(
            conv.astype(BF16), proj[:, cols], (((1,), (1,)), ((), ())), preferred_element_type=F32
        )
    terms[...] = total.astype(BF16)


def project_call(where, shares, args):
    return call(
        project_kernel,
        "norm_project_conv",
        14,
        [SCALARS] + [HELD] * (4 + len(args)),
        [
            jax.ShapeDtypeStruct((ROWS, CHANNELS), F32),
            jax.ShapeDtypeStruct((ROWS, TERMS), BF16),
            jax.ShapeDtypeStruct((3, SLOTS, CHANNELS), BF16),
        ],
        [
            pltpu.VMEM((4, ROWS, SHARE), BF16),
            pltpu.VMEM((ROWS, FEATURES), BF16),
            pltpu.VMEM((ROWS, CHANNELS), BF16),
        ],
        [where, *shares, *args],
    )


def scan_kernel(final, *refs):
    refs = list(refs)
    take = lambda count: [refs.pop(0) for _ in range(count)]
    (where,) = take(1)
    terms = take(4)
    onehot, keep, cached_scales, pool, conv, start, store, gains = take(8)
    if final:
        scan_out, codes_out, scales_out = take(3)
    else:
        (big,) = take(1)
        kept_out, sent_out = take(2)
    entry, readout, fetched, sizes = take(4)
    if final:
        states, natural, scale_acc = take(3)
    else:
        gated, weight, loaded = take(3)
        parts = [
            pltpu.make_async_copy(
                big.at[pl.ds(b * CB, CB)], weight.at[pl.ds(b * CB, CB)], loaded.at[b]
            )
            for b in range(STEPS)
        ]
        for copy in parts:
            copy.start()
    used = ROWS if final else 2 * SLOTS

    def gate(t, cols):
        first = GATE_ROWS + t * SLOTS
        return store[first : first + SLOTS, cols].astype(F32)

    total = terms[0][...].astype(F32)
    for piece in terms[1:]:
        total = total + piece[...].astype(F32)
    sizes[...] = softplus(
        jnp.dot(
            total[:, :RANK].astype(BF16),
            store[STEP_ROWS : STEP_ROWS + RANK],
            preferred_element_type=F32,
        )
        + gains[OFFSET_ROW : OFFSET_ROW + 1]
    )
    for n in range(STATES):
        e, r = RANK + n, RANK + STATES + n
        entry[n] = jnp.broadcast_to(total[:, e : e + 1], (ROWS, LANES))
        readout[n] = jnp.broadcast_to(total[:, r : r + 1], (ROWS, LANES))
    if final:
        scale_acc[...] = jnp.zeros_like(scale_acc)

    def scan_block(block, carry):
        fetched[...] = jnp.dot(
            onehot[block // 2, :used],
            pool[block, :, :CODE_LANES],
            preferred_element_type=F32,
        )
        for part in range(CB // LANES):
            index = block * (CB // LANES) + part
            scan_tile(index, part)
        return carry

    def scan_tile(index, part):
        cols = tile(index)
        new_scale = column_of(cached_scales[...], index)
        size = [sizes[t * SLOTS : (t + 1) * SLOTS, cols] for t in range(TICKS)]
        conv_now = [conv[t * SLOTS : (t + 1) * SLOTS, cols] for t in range(TICKS)]
        gain = [size[t] * conv_now[t] for t in range(TICKS)]
        total = [gains[SKIP_ROW : SKIP_ROW + 1, cols] * conv_now[t] for t in range(TICKS)]
        arrived_scale = [
            jnp.broadcast_to(new_scale[t * SLOTS : (t + 1) * SLOTS], (SLOTS, LANES))
            for t in range(TICKS - 1)
        ]
        stays = [keep[t * SLOTS : (t + 1) * SLOTS] > 0.5 for t in range(TICKS - 1)]
        square = jnp.zeros((SLOTS, LANES), F32)
        for n in range(STATES):
            rate = gains[DECAY_ROW + n : DECAY_ROW + n + 1, cols] * -LOG2E
            state = start[n, :, cols]
            lanes = slice(n * CB + part * LANES, n * CB + (part + 1) * LANES)
            for t in range(TICKS):
                rows = slice(t * SLOTS, (t + 1) * SLOTS)
                state = jnp.exp2(size[t] * rate) * state + gain[t] * entry[n, rows]
                total[t] = total[t] + readout[n, rows] * state
                if t < TICKS - 1:
                    state = jnp.where(
                        stays[t], state, fetched[rows, lanes] * arrived_scale[t]
                    )
            if final:
                states[n] = state
                square = square + state * state
        if not final:
            for t in range(TICKS):
                rows = slice(t * SLOTS, (t + 1) * SLOTS)
                gated[rows, cols] = (total[t] * silu(gate(t, cols))).astype(BF16)
            return
        for t in range(TICKS):
            scan_out[t * SLOTS : (t + 1) * SLOTS, cols] = total[t].astype(BF16)
        mean = jnp.sum(square, axis=1, keepdims=True) * (1.0 / (STATES * LANES))
        scale = jnp.sqrt(mean + 1e-06).astype(BF16).astype(F32)
        inverse = jnp.broadcast_to(1.0 / scale, (SLOTS, LANES))
        last = slice((TICKS - 1) * SLOTS, TICKS * SLOTS)
        kept = keep[last] > 0.5
        for n in range(STATES):
            lanes = slice(n * CB + part * LANES, n * CB + (part + 1) * LANES)
            natural[pl.ds(n, SLOTS, stride=STATES), :] = jnp.where(
                kept, states[n] * inverse, fetched[last, lanes]
            )
        codes_out[:, :, cols] = natural[...].reshape(SLOTS, STATES, LANES).astype(BF16)
        chosen = jnp.where(kept, jnp.broadcast_to(scale, (SLOTS, LANES)), new_scale[last])
        lane = lax.broadcasted_iota(jnp.int32, (SLOTS, LANES), 1)
        scale_acc[...] = jnp.where(lane == index, chosen, scale_acc[...])

    lax.fori_loop(0, STEPS, scan_block, 0)
    if final:
        scales_out[...] = scale_acc[...].T[: CHANNELS // LANES].astype(BF16)
        return
    for copy in parts:
        copy.wait()
    core = where[1] % 2
    for chip in range(2):
        for offset, out in ((core, kept_out), (1 - core, sent_out)):
            cols = pl.ds(pl.multiple_of((2 * chip + offset) * SHARE, SHARE), SHARE)
            out[chip] = jnp.dot(
                gated[...], weight[:, cols], preferred_element_type=F32
            ).astype(out.dtype)


def scan_call(final, where, terms, args):
    scratch = [
        pltpu.VMEM((STATES, ROWS, LANES), F32),
        pltpu.VMEM((STATES, ROWS, LANES), F32),
        pltpu.VMEM((ROWS if final else 2 * SLOTS, STATES * CB), F32),
        pltpu.VMEM((ROWS, CHANNELS), F32),
    ]
    if final:
        out_shape = [
            jax.ShapeDtypeStruct((ROWS, CHANNELS), BF16),
            jax.ShapeDtypeStruct((SLOTS, STATES, CHANNELS), BF16),
            jax.ShapeDtypeStruct((CHANNELS // LANES, SLOTS), BF16),
        ]
        scratch += [
            pltpu.VMEM((STATES, SLOTS, LANES), F32),
            pltpu.VMEM((SLOTS * STATES, LANES), F32),
            pltpu.VMEM((SLOTS, LANES), F32),
        ]
    else:
        out_shape = [
            jax.ShapeDtypeStruct((2, ROWS, SHARE), F32),
            jax.ShapeDtypeStruct((2, ROWS, SHARE), BF16),
        ]
        scratch += [
            pltpu.VMEM((ROWS, CHANNELS), BF16),
            pltpu.VMEM((CHANNELS, FEATURES), BF16),
            pltpu.SemaphoreType.DMA((STEPS,)),
        ]
    return call(
        functools.partial(scan_kernel, final),
        "scan_final" if final else "scan_gate_project",
        16 if final else 36,
        [SCALARS] + [HELD] * (4 + len(args) - (not final)) + [ANYWHERE] * (not final),
        out_shape,
        scratch,
        [where, *terms, *args],
    )


def chip_kernel(where, kept, got, same, other):
    chip = where[1] // 2
    for place, out in ((chip, same), (1 - chip, other)):
        out[...] = (kept[place] + got[place].astype(F32)).astype(BF16)


def chip_call(where, kept, got):
    share = jax.ShapeDtypeStruct((ROWS, SHARE), BF16)
    return call(
        chip_kernel,
        "sum_on_chip",
        14,
        [SCALARS, HELD, HELD],
        [share, share],
        [],
        [where, kept, got],
    )


def add_kernel(residual, same, other, out):
    total = same[...].astype(F32) + other[...].astype(F32)
    out[...] = (residual[...].astype(F32) + total).astype(BF16)


def add_first_kernel(where, residual, same, other, stream, out):
    @pl.when(where[0] == 0)
    def _():
        add_kernel(residual, same, other, out)

    @pl.when(where[0] == 1)
    def _():
        out[...] = stream[...]


def add_call(kernel, name, args, scalars):
    return call(
        kernel,
        name,
        14,
        [SCALARS] * len(scalars) + [HELD] * len(args),
        [jax.ShapeDtypeStruct((ROWS, SHARE), BF16)],
        [],
        [*scalars, *args],
    )[0]


def exchange(value, step):
    return lax.ppermute(value, "tensor", [(i, i ^ step) for i in range(4)])


def along(value, axis, step):
    if axis == "y":
        pairs = [(i, (i // 4) * 4 + (i + step) % 4) for i in range(16)]
    else:
        pairs = [(i, (i + 4 * step) % 16) for i in range(16)]
    return lax.ppermute(value, "replica", pairs)


def gather_far(near, far):
    first, last = cat_rows(near)
    first_below, last_above = along(first, far, 1), along(last, far, 3)
    last_below, first_above = along(last, far, 1), along(first, far, 3)
    first_far, last_far = along(first_below, far, 1), along(last_above, far, 3)
    return [first, first_below, first_far, first_above, last, last_below, last_far, last_above]


def in_section_one(value, step):
    pairs = [(4 + i, 4 + (i ^ step)) for i in range(4)]
    return lax.ppermute(value, ("section", "tensor"), pairs)


def local(
    inner_input,
    gate_input,
    residual,
    projection,
    state_proj,
    step_proj,
    conv_weight,
    conv_bias,
    decay_rate,
    skip_gain,
    step_bias,
    norm_gain,
    state_codes,
    state_scales,
    conv_window,
    cache_codes,
    cache_scales,
    cache_window,
    finished,
    refill_source,
):
    section = lax.axis_index("section")
    column = lax.axis_index("tensor")
    replica = lax.axis_index("replica")
    where = jnp.stack([section, column, replica // 4, replica % 4]).astype(jnp.int32)

    rows = cache_window.shape[1]
    cached = arrange_call(cache_codes[0], cache_window[0].transpose(1, 0, 2), cache_scales[0])

    gains = jnp.concatenate(
        [conv_weight[0], conv_bias, decay_rate[0], skip_gain, step_bias], axis=0
    )
    near_a = [cached[0]] + [along(cached[0], "y", k) for k in (1, 2, 3)]
    near_b = [cached[1]] + [along(cached[1], "z", k) for k in (1, 2, 3)]
    near_a, near_b, gains, proj = lax.optimization_barrier(
        (near_a, near_b, gains, state_proj[0].T)
    )
    pieces = gather_far(near_a, "z") + gather_far(near_b, "y")

    sources = lax.dynamic_slice_in_dim(refill_source, replica * SLOTS, SLOTS, 1)
    room = ((0, 0), (0, LANES - ROWS))
    sources = jnp.pad(sources.reshape(1, ROWS), room, constant_values=-1)
    ended = jnp.pad(finished.reshape(1, ROWS), room)

    small = (sources, ended, where, residual.reshape(ROWS, FEATURES), norm_gain[None])
    flat = (
        step_proj[0],
        inner_input.reshape(ROWS, CHANNELS),
        gate_input.reshape(ROWS, CHANNELS),
        conv_window[0].transpose(1, 0, 2).reshape(ROWS, CHANNELS),
    )
    small, flat, codes, weight, pieces[0], pieces[8] = lax.optimization_barrier(
        (small, flat, state_codes[0], projection[0], pieces[0], pieces[8])
    )
    sources, ended, where, residual_rows, gain = small
    onehot, keep = plan_call(where, sources, ended)
    store = fill_call("hold_store", list(flat))
    states = unfold_call(codes, state_scales[0])
    column_share = lax.dynamic_slice_in_dim(residual_rows, column * SHARE, SHARE, 1)
    states, store, onehot, keep, pieces = lax.optimization_barrier(
        (states, store, onehot, keep, pieces)
    )
    pool = pool_call(pieces)

    conv_out, terms, cached_scales, taken = conv_call(
        (store, onehot, keep, gains, proj, pool)
    )
    all_terms = [terms] + [exchange(terms, k) for k in (1, 2, 3)]
    shared = (onehot, keep, cached_scales, pool)
    layer = (states, store, gains)
    kept, sent = scan_call(False, where, all_terms, (*shared, conv_out, *layer, weight))

    same, other = chip_call(where, kept, exchange(sent, 1))
    big, same, other = lax.optimization_barrier((weight, same, other))
    big = fill_call("hold_projection", [big])
    other_far = lax.ppermute(other, ("section", "tensor"), [(i, (i + 4) % 8 ^ 2) for i in range(8)])
    same_far = lax.ppermute(same, "section", [(0, 1), (1, 0)])
    big, same_far, other_far = lax.optimization_barrier((big, same_far, other_far))
    stream = add_call(add_kernel, "add_residual", (column_share, same_far, other_far), ())
    other, stream = lax.optimization_barrier((other, stream))
    got_a = in_section_one(stream, 2)
    got_b = in_section_one(stream, 1)
    got_c = in_section_one(got_a, 1)
    other = exchange(other, 2)

    conv_out, terms, window_out = project_call(
        where, (stream, got_a, got_b, got_c), (gain, store, keep, gains, proj, taken, big)
    )
    all_terms = [terms] + [exchange(terms, k) for k in (1, 2, 3)]
    other, conv_out = lax.optimization_barrier((other, conv_out))
    stream = add_call(
        add_first_kernel, "add_first", (column_share, same, other, stream), (where,)
    )
    window_out, stream, conv_out = lax.optimization_barrier(
        (window_out.transpose(1, 0, 2), stream, conv_out)
    )
    scan_out, codes_out, scales_out = scan_call(
        True, where, all_terms, (*shared, conv_out, *layer)
    )
    return (
        stream.reshape(TICKS, SLOTS, SHARE),
        scan_out.reshape(1, TICKS, SLOTS, CHANNELS),
        codes_out[None],
        scales_out.T[None],
        window_out[None],
    )


def solution(mesh):
    return jax.shard_map(
        local,
        mesh=mesh,
        in_specs=(
            P(None, "replica", "tensor"),
            P(None, "replica", "tensor"),
            P(None, "replica", None),
            P("section", "tensor", None),
            P("section", "tensor", None),
            P("section", None, "tensor"),
            P("section", None, "tensor"),
            P("section", "tensor"),
            P("section", None, "tensor"),
            P("section", "tensor"),
            P("section", "tensor"),
            P(),
            P("section", "replica", None, "tensor"),
            P("section", "replica", "tensor"),
            P("section", "replica", None, "tensor"),
            P("section", "replica", None, "tensor"),
            P("section", "replica", "tensor"),
            P("section", "replica", None, "tensor"),
            P(None, "replica"),
            P(),
        ),
        out_specs=(
            P(None, "replica", "tensor"),
            P("section", None, "replica", "tensor"),
            P("section", "replica", None, "tensor"),
            P("section", "replica", "tensor"),
            P("section", "replica", None, "tensor"),
        ),
        check_vma=False,
    )
```

```python
import functools
import math

import jax
import jax.numpy as jnp
from jax import lax
from jax.experimental import pallas as pl
from jax.experimental.pallas import tpu as pltpu
from jax.sharding import PartitionSpec as P

RANK = 256
STATES = 16
TICKS = 3
SLOTS = 32
ROWS = TICKS * SLOTS
CHANNELS = 2048
FEATURES = 4096
SHARE = FEATURES // 4
CB = 512
STEPS = CHANNELS // CB
LANES = 128
TERMS = RANK + 2 * STATES
POOL = 64
WIDE = 4 * CB
CODE_LANES = STATES * CB
GROUP = CODE_LANES + WIDE
LOG2E = math.log2(math.e)
F32 = jnp.float32
BF16 = jnp.bfloat16
MIB = 1024 * 1024
COST = pl.CostEstimate(flops=1, transcendentals=0, bytes_accessed=1)


HELD = pl.BlockSpec(memory_space=pltpu.VMEM)
SCALARS = pl.BlockSpec(memory_space=pltpu.SMEM)
ANYWHERE = pl.BlockSpec(memory_space=pltpu.HBM)


def held(shape, dtype):
    return pltpu.VMEM(shape, dtype)


def call(kernel, name, mebibytes, in_specs, out_shape, scratch, args, out_specs=None):
    if out_specs is None:
        out_specs = [HELD] * len(out_shape) if isinstance(out_shape, list) else HELD
    return pl.pallas_call(
        kernel,
        in_specs=in_specs,
        out_specs=out_specs,
        out_shape=out_shape,
        scratch_shapes=scratch,
        compiler_params=pltpu.CompilerParams(vmem_limit_bytes=mebibytes * MIB),
        cost_estimate=COST,
        name=name,
    )(*args)


def cat_kernel(*refs):
    sources, outs, held, left = refs[:8], refs[8:12], refs[12], refs[13]
    copies = []
    for half in range(2):
        for block in range(2):
            cols = slice(block * GROUP, (block + 1) * GROUP)
            place = 2 * half + block
            held[place] = jnp.concatenate(
                [source[:, cols] for source in sources[4 * half : 4 * half + 4]], axis=0
            )
            copies.append(
                pltpu.make_async_copy(held.at[place], outs[place], left.at[place])
            )
            copies[-1].start()
    for copy in copies:
        copy.wait()


def cat_rows(pieces):
    return call(
        cat_kernel,
        "cat_rows",
        60,
        [HELD] * 8,
        [jax.ShapeDtypeStruct((16, GROUP), BF16)] * 4,
        [pltpu.VMEM((4, 16, GROUP), BF16), pltpu.SemaphoreType.DMA((4,))],
        pieces,
        [ANYWHERE] * 4,
    )


def silu(x):
    return x / (1.0 + jnp.exp(-x))


def softplus(x):
    return jnp.maximum(x, 0.0) + jnp.log1p(jnp.exp(-jnp.abs(x)))


def column_of(table, lane):
    index = lax.broadcasted_iota(jnp.int32, table.shape, 1)
    return jnp.sum(jnp.where(index == lane, table, 0.0), axis=1, keepdims=True)


def tile(index):
    return pl.ds(pl.multiple_of(index * LANES, LANES), LANES)


def fill_kernel(*refs):
    sources, target, arrived = refs[:-2], refs[-2], refs[-1]
    copies, row = [], 0
    for i, source in enumerate(sources):
        count = source.shape[0]
        copies.append(
            pltpu.make_async_copy(source, target.at[pl.ds(row, count)], arrived.at[i])
        )
        copies[-1].start()
        row += count
    for copy in copies:
        copy.wait()


def fill_call(name, arrays):
    rows = sum(array.shape[0] for array in arrays)
    return call(
        fill_kernel,
        name,
        14,
        [ANYWHERE] * len(arrays),
        held((rows, arrays[0].shape[1]), BF16),
        [pltpu.SemaphoreType.DMA((len(arrays),))],
        arrays,
    )


def arrange_kernel(codes, windows, scales, first, last, code_rows, window_rows):
    rows = codes.shape[0]
    for part in range(CHANNELS // LANES):
        code_rows[part] = (
            codes[:, :, part * LANES : (part + 1) * LANES]
            .astype(F32)
            .reshape(rows * STATES, LANES)
        )
    for k in range(3):
        window_rows[k * 8 : k * 8 + rows] = windows[k].astype(F32)
    for block in range(STEPS):
        out = (first, last)[block // 2]
        base = block % 2 * GROUP
        cols = slice(block * CB, (block + 1) * CB)
        for n in range(STATES):
            for part in range(CB // LANES):
                lanes = slice(base + n * CB + part * LANES, base + n * CB + (part + 1) * LANES)
                out[:, lanes] = code_rows[
                    block * (CB // LANES) + part, pl.ds(n, rows, stride=STATES), :
                ].astype(BF16)
        base += CODE_LANES
        for k in range(3):
            out[:, base + k * CB : base + (k + 1) * CB] = window_rows[
                k * 8 : k * 8 + rows, cols
            ].astype(BF16)
        out[:, base + 3 * CB : base + 4 * CB] = jnp.zeros((rows, CB), BF16)
        out[:, base + 3 * CB : base + 3 * CB + scales.shape[1]] = scales[...]


def arrange_call(codes, windows, scales):
    rows = codes.shape[0]
    half = jax.ShapeDtypeStruct((rows, STEPS // 2 * GROUP), BF16)
    return call(
        arrange_kernel,
        "arrange_rows",
        60,
        [HELD] * 3,
        [half, half],
        [
            pltpu.VMEM((CHANNELS // LANES, rows * STATES, LANES), F32),
            pltpu.VMEM((24, CHANNELS), F32),
        ],
        [codes, windows, scales],
    )


def plan_kernel(where, sources, ended, onehot, keep):
    source, over = sources[...], ended[...]
    owner, within = source >> 2, source & 3
    z = (where[2] - (owner >> 2)) & 3
    y = (where[3] - (owner & 3)) & 3
    taken = (source >= 0) & (over == 1)
    row = lax.broadcasted_iota(jnp.int32, (POOL, LANES), 0)
    for half, place in enumerate((z * 16 + y * 4 + within, y * 16 + z * 4 + within)):
        place = jnp.where(taken, place, -1)
        chosen = jnp.where(row == place, 1.0, 0.0).astype(F32)
        onehot[half] = chosen.T[:ROWS].astype(BF16)
    stays = jnp.where(over == 1, 0.0, 1.0).astype(F32)
    keep[...] = jnp.broadcast_to(stays, (LANES, LANES)).T[:ROWS]


def plan_call(where, sources, ended):
    return call(
        plan_kernel,
        "plan_rows",
        14,
        [SCALARS, HELD, HELD],
        [
            jax.ShapeDtypeStruct((2, ROWS, POOL), BF16),
            jax.ShapeDtypeStruct((ROWS, LANES), F32),
        ],
        [],
        [where, sources, ended],
    )


def unfold_kernel(codes, scales, states, natural):
    def unfold(block, carry):
        cols = tile(block)
        natural[...] = codes[:, :, cols].astype(F32).reshape(SLOTS * STATES, LANES)
        scale = jnp.broadcast_to(column_of(scales[...].astype(F32), block), (SLOTS, LANES))
        for n in range(STATES):
            states[n, :, cols] = natural[pl.ds(n, SLOTS, stride=STATES), :] * scale
        return carry

    lax.fori_loop(0, CHANNELS // LANES, unfold, 0)


def unfold_call(codes, scales):
    return call(
        unfold_kernel,
        "unfold_states",
        14,
        [HELD] * 2,
        held((STATES, SLOTS, CHANNELS), F32),
        [pltpu.VMEM((SLOTS * STATES, LANES), F32)],
        [codes, scales],
    )


def pool_kernel(*refs):
    pieces, pool, arrived = refs[: 4 * STEPS], refs[-2], refs[-1]
    copies = [
        pltpu.make_async_copy(piece, pool.at[i // 4, pl.ds(i % 4 * 16, 16)], arrived.at[i])
        for i, piece in enumerate(pieces)
    ]
    for copy in copies:
        copy.start()
    for copy in copies:
        copy.wait()


def pool_call(pieces):
    return call(
        pool_kernel,
        "pool_rows",
        50,
        [ANYWHERE] * (4 * STEPS),
        held((STEPS, POOL, GROUP), BF16),
        [pltpu.SemaphoreType.DMA((4 * STEPS,))],
        pieces,
    )


STEP_ROWS, INPUT_ROWS, GATE_ROWS, WINDOW_ROWS = 0, RANK, RANK + ROWS, RANK + 2 * ROWS
TAP_ROW, BIAS_ROW, DECAY_ROW, SKIP_ROW, OFFSET_ROW = 0, 4, 5, 21, 22


def conv_block(inputs, store, fetched, keep, gains, cols):
    past = [
        store[WINDOW_ROWS + k * SLOTS : WINDOW_ROWS + (k + 1) * SLOTS, cols].astype(F32)
        for k in range(3)
    ]
    outs = []
    for tick in range(TICKS):
        rows = slice(tick * SLOTS, (tick + 1) * SLOTS)
        taps = past + [inputs[rows].astype(F32)]
        total = gains[BIAS_ROW : BIAS_ROW + 1, cols]
        for k in range(4):
            total = total + gains[TAP_ROW + k : TAP_ROW + k + 1, cols] * taps[k]
        outs.append(silu(total))
        stays = keep[rows, :1] > 0.5
        past = [jnp.where(stays, taps[k + 1], fetched(k, rows)) for k in range(3)]
    return jnp.concatenate(outs, axis=0), past


def conv_kernel(
    store, onehot, keep, gains, proj, pool, conv_out, terms, scales, taken_out, taken, left, conv_held, gone
):
    copies = []
    total = jnp.zeros((ROWS, TERMS), F32)
    for block in range(STEPS):
        cols = slice(block * CB, (block + 1) * CB)
        fetched = jnp.dot(
            onehot[block // 2], pool[block, :, CODE_LANES:], preferred_element_type=F32
        )
        if block == 0:
            scales[...] = fetched[:, 3 * CB : 3 * CB + LANES]
        for k in range(3):
            taken[block, k] = fetched[:, k * CB : (k + 1) * CB].astype(BF16)
        copies.append(
            pltpu.make_async_copy(taken.at[block], taken_out.at[block], left.at[block])
        )
        copies[-1].start()
        inputs = store[INPUT_ROWS : INPUT_ROWS + ROWS, cols]
        conv, _ = conv_block(
            inputs, store, lambda k, rows: fetched[rows, k * CB : (k + 1) * CB], keep, gains, cols
        )
        conv_held[block] = conv
        copies.append(
            pltpu.make_async_copy(
                conv_held.at[block], conv_out.at[:, pl.ds(block * CB, CB)], gone.at[block]
            )
        )
        copies[-1].start()
        total = total + lax.dot_general(
            conv.astype(BF16), proj[:, cols], (((1,), (1,)), ((), ())), preferred_element_type=F32
        )
    terms[...] = total.astype(BF16)
    for copy in copies:
        copy.wait()


def conv_call(args):
    return call(
        conv_kernel,
        "conv_terms",
        14,
        [HELD] * len(args),
        [
            jax.ShapeDtypeStruct((ROWS, CHANNELS), F32),
            jax.ShapeDtypeStruct((ROWS, TERMS), BF16),
            jax.ShapeDtypeStruct((ROWS, LANES), F32),
            jax.ShapeDtypeStruct((STEPS, 3, ROWS, CB), BF16),
        ],
        [
            pltpu.VMEM((STEPS, 3, ROWS, CB), BF16),
            pltpu.SemaphoreType.DMA((STEPS,)),
            pltpu.VMEM((STEPS, ROWS, CB), F32),
            pltpu.SemaphoreType.DMA((STEPS,)),
        ],
        args,
        [ANYWHERE, HELD, HELD, ANYWHERE],
    )


def project_kernel(
    where,
    s_own,
    s_a,
    s_b,
    s_c,
    gain,
    store,
    keep,
    gains,
    proj,
    taken,
    big,
    conv_out,
    terms,
    win_out,
    values,
    normed,
    entering,
):
    section, column = where[0], where[1]

    @pl.when(section == 0)
    def _():
        entering[...] = store[INPUT_ROWS : INPUT_ROWS + ROWS]

    @pl.when(section == 1)
    def _():
        values[column] = s_own[...]
        values[column ^ 2] = s_a[...]
        values[column ^ 1] = s_b[...]
        values[column ^ 3] = s_c[...]
        total = jnp.zeros((ROWS, 1), F32)
        for f in range(4):
            v = values[f].astype(F32)
            total = total + jnp.sum(v * v, axis=1, keepdims=True)
        factor = lax.rsqrt(total * (1.0 / FEATURES) + 1e-05)
        for f in range(4):
            cols = slice(f * SHARE, (f + 1) * SHARE)
            v = values[f].astype(F32)
            normed[:, cols] = (v * factor * gain[:, cols].astype(F32)).astype(BF16)

    total = jnp.zeros((ROWS, TERMS), F32)
    for block in range(STEPS):
        cols = slice(block * CB, (block + 1) * CB)

        @pl.when(section == 1)
        def _():
            entering[:, cols] = lax.dot_general(
                normed[...], big[cols], (((1,), (1,)), ((), ())), preferred_element_type=F32
            ).astype(BF16)

        conv, past = conv_block(
            entering[:, cols],
            store,
            lambda k, rows: taken[block, k, rows].astype(F32),
            keep,
            gains,
            cols,
        )
        conv_out[:, cols] = conv
        for k in range(3):
            win_out[k, :, cols] = past[k].astype(BF16)
        total = total + lax.dot_general(
            conv.astype(BF16), proj[:, cols], (((1,), (1,)), ((), ())), preferred_element_type=F32
        )
    terms[...] = total.astype(BF16)


def project_call(where, shares, args):
    return call(
        project_kernel,
        "norm_project_conv",
        14,
        [SCALARS] + [HELD] * (4 + len(args)),
        [
            jax.ShapeDtypeStruct((ROWS, CHANNELS), F32),
            jax.ShapeDtypeStruct((ROWS, TERMS), BF16),
            jax.ShapeDtypeStruct((3, SLOTS, CHANNELS), BF16),
        ],
        [
            pltpu.VMEM((4, ROWS, SHARE), BF16),
            pltpu.VMEM((ROWS, FEATURES), BF16),
            pltpu.VMEM((ROWS, CHANNELS), BF16),
        ],
        [where, *shares, *args],
    )


def scan_kernel(final, *refs):
    refs = list(refs)
    take = lambda count: [refs.pop(0) for _ in range(count)]
    (where,) = take(1)
    terms = take(4)
    onehot, keep, cached_scales, pool, conv, start, store, gains = take(8)
    if final:
        scan_out, codes_out, scales_out = take(3)
    else:
        (big,) = take(1)
        kept_out, sent_out = take(2)
    entry, readout, fetched, sizes = take(4)
    if final:
        states, natural, scale_acc = take(3)
    else:
        gated, weight, loaded = take(3)
        parts = [
            pltpu.make_async_copy(
                big.at[pl.ds(b * CB, CB)], weight.at[pl.ds(b * CB, CB)], loaded.at[b]
            )
            for b in range(STEPS)
        ]
        for copy in parts:
            copy.start()
    used = ROWS if final else 2 * SLOTS

    def gate(t, cols):
        first = GATE_ROWS + t * SLOTS
        return store[first : first + SLOTS, cols].astype(F32)

    total = terms[0][...].astype(F32)
    for piece in terms[1:]:
        total = total + piece[...].astype(F32)
    sizes[...] = softplus(
        jnp.dot(
            total[:, :RANK].astype(BF16),
            store[STEP_ROWS : STEP_ROWS + RANK],
            preferred_element_type=F32,
        )
        + gains[OFFSET_ROW : OFFSET_ROW + 1]
    )
    for n in range(STATES):
        e, r = RANK + n, RANK + STATES + n
        entry[n] = jnp.broadcast_to(total[:, e : e + 1], (ROWS, LANES))
        readout[n] = jnp.broadcast_to(total[:, r : r + 1], (ROWS, LANES))
    if final:
        scale_acc[...] = jnp.zeros_like(scale_acc)

    def scan_block(block, carry):
        fetched[...] = jnp.dot(
            onehot[block // 2, :used],
            pool[block, :, :CODE_LANES],
            preferred_element_type=F32,
        )
        for part in range(CB // LANES):
            index = block * (CB // LANES) + part
            scan_tile(index, part)
        return carry

    def scan_tile(index, part):
        cols = tile(index)
        new_scale = column_of(cached_scales[...], index)
        size = [sizes[t * SLOTS : (t + 1) * SLOTS, cols] for t in range(TICKS)]
        conv_now = [conv[t * SLOTS : (t + 1) * SLOTS, cols] for t in range(TICKS)]
        gain = [size[t] * conv_now[t] for t in range(TICKS)]
        total = [gains[SKIP_ROW : SKIP_ROW + 1, cols] * conv_now[t] for t in range(TICKS)]
        arrived_scale = [
            jnp.broadcast_to(new_scale[t * SLOTS : (t + 1) * SLOTS], (SLOTS, LANES))
            for t in range(TICKS - 1)
        ]
        stays = [keep[t * SLOTS : (t + 1) * SLOTS] > 0.5 for t in range(TICKS - 1)]
        square = jnp.zeros((SLOTS, LANES), F32)
        for n in range(STATES):
            rate = gains[DECAY_ROW + n : DECAY_ROW + n + 1, cols] * -LOG2E
            state = start[n, :, cols]
            lanes = slice(n * CB + part * LANES, n * CB + (part + 1) * LANES)
            for t in range(TICKS):
                rows = slice(t * SLOTS, (t + 1) * SLOTS)
                state = jnp.exp2(size[t] * rate) * state + gain[t] * entry[n, rows]
                total[t] = total[t] + readout[n, rows] * state
                if t < TICKS - 1:
                    state = jnp.where(
                        stays[t], state, fetched[rows, lanes] * arrived_scale[t]
                    )
            if final:
                states[n] = state
                square = square + state * state
        if not final:
            for t in range(TICKS):
                rows = slice(t * SLOTS, (t + 1) * SLOTS)
                gated[rows, cols] = (total[t] * silu(gate(t, cols))).astype(BF16)
            return
        for t in range(TICKS):
            scan_out[t * SLOTS : (t + 1) * SLOTS, cols] = total[t].astype(BF16)
        mean = jnp.sum(square, axis=1, keepdims=True) * (1.0 / (STATES * LANES))
        scale = jnp.sqrt(mean + 1e-06).astype(BF16).astype(F32)
        inverse = jnp.broadcast_to(1.0 / scale, (SLOTS, LANES))
        last = slice((TICKS - 1) * SLOTS, TICKS * SLOTS)
        kept = keep[last] > 0.5
        for n in range(STATES):
            lanes = slice(n * CB + part * LANES, n * CB + (part + 1) * LANES)
            natural[pl.ds(n, SLOTS, stride=STATES), :] = jnp.where(
                kept, states[n] * inverse, fetched[last, lanes]
            )
        codes_out[:, :, cols] = natural[...].reshape(SLOTS, STATES, LANES).astype(BF16)
        chosen = jnp.where(kept, jnp.broadcast_to(scale, (SLOTS, LANES)), new_scale[last])
        lane = lax.broadcasted_iota(jnp.int32, (SLOTS, LANES), 1)
        scale_acc[...] = jnp.where(lane == index, chosen, scale_acc[...])

    lax.fori_loop(0, STEPS, scan_block, 0)
    if final:
        scales_out[...] = scale_acc[...].T[: CHANNELS // LANES].astype(BF16)
        return
    for copy in parts:
        copy.wait()
    core = where[1] % 2
    for chip in range(2):
        for offset, out in ((core, kept_out), (1 - core, sent_out)):
            cols = pl.ds(pl.multiple_of((2 * chip + offset) * SHARE, SHARE), SHARE)
            out[chip] = jnp.dot(
                gated[...], weight[:, cols], preferred_element_type=F32
            ).astype(out.dtype)


def scan_call(final, where, terms, args):
    scratch = [
        pltpu.VMEM((STATES, ROWS, LANES), F32),
        pltpu.VMEM((STATES, ROWS, LANES), F32),
        pltpu.VMEM((ROWS if final else 2 * SLOTS, STATES * CB), F32),
        pltpu.VMEM((ROWS, CHANNELS), F32),
    ]
    if final:
        out_shape = [
            jax.ShapeDtypeStruct((ROWS, CHANNELS), BF16),
            jax.ShapeDtypeStruct((SLOTS, STATES, CHANNELS), BF16),
            jax.ShapeDtypeStruct((CHANNELS // LANES, SLOTS), BF16),
        ]
        scratch += [
            pltpu.VMEM((STATES, SLOTS, LANES), F32),
            pltpu.VMEM((SLOTS * STATES, LANES), F32),
            pltpu.VMEM((SLOTS, LANES), F32),
        ]
    else:
        out_shape = [
            jax.ShapeDtypeStruct((2, ROWS, SHARE), F32),
            jax.ShapeDtypeStruct((2, ROWS, SHARE), BF16),
        ]
        scratch += [
            pltpu.VMEM((ROWS, CHANNELS), BF16),
            pltpu.VMEM((CHANNELS, FEATURES), BF16),
            pltpu.SemaphoreType.DMA((STEPS,)),
        ]
    return call(
        functools.partial(scan_kernel, final),
        "scan_final" if final else "scan_gate_project",
        16 if final else 36,
        [SCALARS] + [HELD] * (4 + len(args) - (not final)) + [ANYWHERE] * (not final),
        out_shape,
        scratch,
        [where, *terms, *args],
    )


def chip_kernel(where, kept, got, same, other):
    chip = where[1] // 2
    for place, out in ((chip, same), (1 - chip, other)):
        out[...] = (kept[place] + got[place].astype(F32)).astype(BF16)


def chip_call(where, kept, got):
    share = jax.ShapeDtypeStruct((ROWS, SHARE), BF16)
    return call(
        chip_kernel,
        "sum_on_chip",
        14,
        [SCALARS, HELD, HELD],
        [share, share],
        [],
        [where, kept, got],
    )


def add_kernel(residual, same, other, out):
    total = same[...].astype(F32) + other[...].astype(F32)
    out[...] = (residual[...].astype(F32) + total).astype(BF16)


def add_first_kernel(where, residual, same, other, stream, out):
    @pl.when(where[0] == 0)
    def _():
        add_kernel(residual, same, other, out)

    @pl.when(where[0] == 1)
    def _():
        out[...] = stream[...]


def add_call(kernel, name, args, scalars):
    return call(
        kernel,
        name,
        14,
        [SCALARS] * len(scalars) + [HELD] * len(args),
        [jax.ShapeDtypeStruct((ROWS, SHARE), BF16)],
        [],
        [*scalars, *args],
    )[0]


def exchange(value, step):
    return lax.ppermute(value, "tensor", [(i, i ^ step) for i in range(4)])


def along(value, axis, step):
    if axis == "y":
        pairs = [(i, (i // 4) * 4 + (i + step) % 4) for i in range(16)]
    else:
        pairs = [(i, (i + 4 * step) % 16) for i in range(16)]
    return lax.ppermute(value, "replica", pairs)


def gather_far(first, last, far):
    first_below, last_above = along(first, far, 1), along(last, far, 3)
    last_below, first_above = along(last, far, 1), along(first, far, 3)
    first_far, last_far = along(first_below, far, 1), along(last_above, far, 3)
    return [first, first_below, first_far, first_above, last, last_below, last_far, last_above]


def in_section_one(value, step):
    pairs = [(4 + i, 4 + (i ^ step)) for i in range(4)]
    return lax.ppermute(value, ("section", "tensor"), pairs)


def local(
    inner_input,
    gate_input,
    residual,
    projection,
    state_proj,
    step_proj,
    conv_weight,
    conv_bias,
    decay_rate,
    skip_gain,
    step_bias,
    norm_gain,
    state_codes,
    state_scales,
    conv_window,
    cache_codes,
    cache_scales,
    cache_window,
    finished,
    refill_source,
):
    section = lax.axis_index("section")
    column = lax.axis_index("tensor")
    replica = lax.axis_index("replica")
    where = jnp.stack([section, column, replica // 4, replica % 4]).astype(jnp.int32)

    rows = cache_window.shape[1]
    cached = arrange_call(cache_codes[0], cache_window[0].transpose(1, 0, 2), cache_scales[0])

    near_a = [cached[0]] + [along(cached[0], "y", k) for k in (1, 2, 3)]
    near_b = [cached[1]] + [along(cached[1], "z", k) for k in (1, 2, 3)]
    near_a, near_b = lax.optimization_barrier((near_a, near_b))
    proj = state_proj[0].T
    first_a, last_a, first_b, last_b = cat_rows(near_a + near_b)

    raw = (refill_source, finished, norm_gain, conv_weight, conv_bias, decay_rate)
    raw = (*raw, skip_gain, step_bias, residual, state_scales)
    raw, first_a, last_a = lax.optimization_barrier((raw, first_a, last_a))
    refill_source, finished, norm_gain, conv_weight, conv_bias, decay_rate = raw[:6]
    skip_gain, step_bias, residual, state_scales = raw[6:]
    gains = jnp.concatenate(
        [conv_weight[0], conv_bias, decay_rate[0], skip_gain, step_bias], axis=0
    )

    sources = lax.dynamic_slice_in_dim(refill_source, replica * SLOTS, SLOTS, 1)
    room = ((0, 0), (0, LANES - ROWS))
    sources = jnp.pad(sources.reshape(1, ROWS), room, constant_values=-1)
    ended = jnp.pad(finished.reshape(1, ROWS), room)

    small = (sources, ended, where, residual.reshape(ROWS, FEATURES), norm_gain[None])
    flat = (
        step_proj[0],
        inner_input.reshape(ROWS, CHANNELS),
        gate_input.reshape(ROWS, CHANNELS),
        conv_window[0].transpose(1, 0, 2).reshape(ROWS, CHANNELS),
    )
    flat, codes, weight, first_b = lax.optimization_barrier(
        (flat, state_codes[0], projection[0], first_b)
    )
    sources, ended, where, residual_rows, gain = small
    onehot, keep = plan_call(where, sources, ended)
    store = fill_call("hold_store", list(flat))
    states = unfold_call(codes, state_scales[0])
    column_share = lax.dynamic_slice_in_dim(residual_rows, column * SHARE, SHARE, 1)
    pieces = gather_far(first_a, last_a, "z") + gather_far(first_b, last_b, "y")
    states, store, onehot, keep, gains, gain, pieces = lax.optimization_barrier(
        (states, store, onehot, keep, gains, gain, pieces)
    )
    pool = pool_call(pieces)

    conv_out, terms, cached_scales, taken = conv_call(
        (store, onehot, keep, gains, proj, pool)
    )
    all_terms = [terms] + [exchange(terms, k) for k in (1, 2, 3)]
    shared = (onehot, keep, cached_scales, pool)
    layer = (states, store, gains)
    kept, sent = scan_call(False, where, all_terms, (*shared, conv_out, *layer, weight))

    same, other = chip_call(where, kept, exchange(sent, 1))
    big, same, other = lax.optimization_barrier((weight, same, other))
    big = fill_call("hold_projection", [big])
    other_far = lax.ppermute(other, ("section", "tensor"), [(i, (i + 4) % 8 ^ 2) for i in range(8)])
    same_far = lax.ppermute(same, "section", [(0, 1), (1, 0)])
    big, same_far, other_far = lax.optimization_barrier((big, same_far, other_far))
    stream = add_call(add_kernel, "add_residual", (column_share, same_far, other_far), ())
    other, stream = lax.optimization_barrier((other, stream))
    got_a = in_section_one(stream, 2)
    got_b = in_section_one(stream, 1)
    got_c = in_section_one(got_a, 1)
    other = exchange(other, 2)

    conv_out, terms, window_out = project_call(
        where, (stream, got_a, got_b, got_c), (gain, store, keep, gains, proj, taken, big)
    )
    all_terms = [terms] + [exchange(terms, k) for k in (1, 2, 3)]
    other, conv_out = lax.optimization_barrier((other, conv_out))
    stream = add_call(
        add_first_kernel, "add_first", (column_share, same, other, stream), (where,)
    )
    window_out, stream, conv_out = lax.optimization_barrier(
        (window_out.transpose(1, 0, 2), stream, conv_out)
    )
    scan_out, codes_out, scales_out = scan_call(
        True, where, all_terms, (*shared, conv_out, *layer)
    )
    return (
        stream.reshape(TICKS, SLOTS, SHARE),
        scan_out.reshape(1, TICKS, SLOTS, CHANNELS),
        codes_out[None],
        scales_out.T[None],
        window_out[None],
    )


def solution(mesh):
    return jax.shard_map(
        local,
        mesh=mesh,
        in_specs=(
            P(None, "replica", "tensor"),
            P(None, "replica", "tensor"),
            P(None, "replica", None),
            P("section", "tensor", None),
            P("section", "tensor", None),
            P("section", None, "tensor"),
            P("section", None, "tensor"),
            P("section", "tensor"),
            P("section", None, "tensor"),
            P("section", "tensor"),
            P("section", "tensor"),
            P(),
            P("section", "replica", None, "tensor"),
            P("section", "replica", "tensor"),
            P("section", "replica", None, "tensor"),
            P("section", "replica", None, "tensor"),
            P("section", "replica", "tensor"),
            P("section", "replica", None, "tensor"),
            P(None, "replica"),
            P(),
        ),
        out_specs=(
            P(None, "replica", "tensor"),
            P("section", None, "replica", "tensor"),
            P("section", "replica", None, "tensor"),
            P("section", "replica", "tensor"),
            P("section", "replica", None, "tensor"),
        ),
        check_vma=False,
    )
```

```python
import functools
import math

import jax
import jax.numpy as jnp
from jax import lax
from jax.experimental import pallas as pl
from jax.experimental.pallas import tpu as pltpu
from jax.sharding import PartitionSpec as P

RANK = 256
STATES = 16
TICKS = 3
SLOTS = 32
ROWS = TICKS * SLOTS
CHANNELS = 2048
FEATURES = 4096
SHARE = FEATURES // 4
CB = 512
STEPS = CHANNELS // CB
LANES = 128
TERMS = RANK + 2 * STATES
POOL = 64
WIDE = 4 * CB
CODE_LANES = STATES * CB
GROUP = CODE_LANES + WIDE
LOG2E = math.log2(math.e)
F32 = jnp.float32
BF16 = jnp.bfloat16
MIB = 1024 * 1024
COST = pl.CostEstimate(flops=1, transcendentals=0, bytes_accessed=1)


HELD = pl.BlockSpec(memory_space=pltpu.VMEM)
SCALARS = pl.BlockSpec(memory_space=pltpu.SMEM)
ANYWHERE = pl.BlockSpec(memory_space=pltpu.HBM)


def held(shape, dtype):
    return pltpu.VMEM(shape, dtype)


def call(kernel, name, mebibytes, in_specs, out_shape, scratch, args, out_specs=None):
    if out_specs is None:
        out_specs = [HELD] * len(out_shape) if isinstance(out_shape, list) else HELD
    return pl.pallas_call(
        kernel,
        in_specs=in_specs,
        out_specs=out_specs,
        out_shape=out_shape,
        scratch_shapes=scratch,
        compiler_params=pltpu.CompilerParams(vmem_limit_bytes=mebibytes * MIB),
        cost_estimate=COST,
        name=name,
    )(*args)


def cat_kernel(*refs):
    sources, outs, held, left = refs[:8], refs[8:12], refs[12], refs[13]
    copies = []
    for half in range(2):
        for block in range(2):
            cols = slice(block * GROUP, (block + 1) * GROUP)
            place = 2 * half + block
            held[place] = jnp.concatenate(
                [source[:, cols] for source in sources[4 * half : 4 * half + 4]], axis=0
            )
            copies.append(
                pltpu.make_async_copy(held.at[place], outs[place], left.at[place])
            )
            copies[-1].start()
    for copy in copies:
        copy.wait()


def cat_rows(pieces):
    return call(
        cat_kernel,
        "cat_rows",
        60,
        [HELD] * 8,
        [jax.ShapeDtypeStruct((16, GROUP), BF16)] * 4,
        [pltpu.VMEM((4, 16, GROUP), BF16), pltpu.SemaphoreType.DMA((4,))],
        pieces,
        [ANYWHERE] * 4,
    )


def silu(x):
    return x / (1.0 + jnp.exp(-x))


def softplus(x):
    return jnp.maximum(x, 0.0) + jnp.log1p(jnp.exp(-jnp.abs(x)))


def column_of(table, lane):
    index = lax.broadcasted_iota(jnp.int32, table.shape, 1)
    return jnp.sum(jnp.where(index == lane, table, 0.0), axis=1, keepdims=True)


def tile(index):
    return pl.ds(pl.multiple_of(index * LANES, LANES), LANES)


def fill_kernel(*refs):
    sources, target, arrived = refs[:-2], refs[-2], refs[-1]
    copies, row = [], 0
    for i, source in enumerate(sources):
        count = source.shape[0]
        copies.append(
            pltpu.make_async_copy(source, target.at[pl.ds(row, count)], arrived.at[i])
        )
        copies[-1].start()
        row += count
    for copy in copies:
        copy.wait()


def fill_call(name, arrays):
    rows = sum(array.shape[0] for array in arrays)
    return call(
        fill_kernel,
        name,
        14,
        [ANYWHERE] * len(arrays),
        held((rows, arrays[0].shape[1]), BF16),
        [pltpu.SemaphoreType.DMA((len(arrays),))],
        arrays,
    )


def arrange_kernel(codes, windows, scales, first, last, code_rows, window_rows):
    rows = codes.shape[0]
    for part in range(CHANNELS // LANES):
        code_rows[part] = (
            codes[:, :, part * LANES : (part + 1) * LANES]
            .astype(F32)
            .reshape(rows * STATES, LANES)
        )
    for k in range(3):
        window_rows[k * 8 : k * 8 + rows] = windows[k].astype(F32)
    for block in range(STEPS):
        out = (first, last)[block // 2]
        base = block % 2 * GROUP
        cols = slice(block * CB, (block + 1) * CB)
        for n in range(STATES):
            for part in range(CB // LANES):
                lanes = slice(base + n * CB + part * LANES, base + n * CB + (part + 1) * LANES)
                out[:, lanes] = code_rows[
                    block * (CB // LANES) + part, pl.ds(n, rows, stride=STATES), :
                ].astype(BF16)
        base += CODE_LANES
        for k in range(3):
            out[:, base + k * CB : base + (k + 1) * CB] = window_rows[
                k * 8 : k * 8 + rows, cols
            ].astype(BF16)
        out[:, base + 3 * CB : base + 4 * CB] = jnp.zeros((rows, CB), BF16)
        out[:, base + 3 * CB : base + 3 * CB + scales.shape[1]] = scales[...]


def arrange_call(codes, windows, scales):
    rows = codes.shape[0]
    half = jax.ShapeDtypeStruct((rows, STEPS // 2 * GROUP), BF16)
    return call(
        arrange_kernel,
        "arrange_rows",
        60,
        [HELD] * 3,
        [half, half],
        [
            pltpu.VMEM((CHANNELS // LANES, rows * STATES, LANES), F32),
            pltpu.VMEM((24, CHANNELS), F32),
        ],
        [codes, windows, scales],
    )


def plan_kernel(where, sources, ended, onehot, keep):
    source, over = sources[...], ended[...]
    owner, within = source >> 2, source & 3
    z = (where[2] - (owner >> 2)) & 3
    y = (where[3] - (owner & 3)) & 3
    taken = (source >= 0) & (over == 1)
    row = lax.broadcasted_iota(jnp.int32, (POOL, LANES), 0)
    for half, place in enumerate((z * 16 + y * 4 + within, y * 16 + z * 4 + within)):
        place = jnp.where(taken, place, -1)
        chosen = jnp.where(row == place, 1.0, 0.0).astype(F32)
        onehot[half] = chosen.T[:ROWS].astype(BF16)
    stays = jnp.where(over == 1, 0.0, 1.0).astype(F32)
    keep[...] = jnp.broadcast_to(stays, (LANES, LANES)).T[:ROWS]


def plan_call(where, sources, ended):
    return call(
        plan_kernel,
        "plan_rows",
        14,
        [SCALARS, HELD, HELD],
        [
            jax.ShapeDtypeStruct((2, ROWS, POOL), BF16),
            jax.ShapeDtypeStruct((ROWS, LANES), F32),
        ],
        [],
        [where, sources, ended],
    )


def unfold_kernel(codes, scales, states, natural):
    def unfold(block, carry):
        cols = tile(block)
        natural[...] = codes[:, :, cols].astype(F32).reshape(SLOTS * STATES, LANES)
        scale = jnp.broadcast_to(column_of(scales[...].astype(F32), block), (SLOTS, LANES))
        for n in range(STATES):
            states[n, :, cols] = natural[pl.ds(n, SLOTS, stride=STATES), :] * scale
        return carry

    lax.fori_loop(0, CHANNELS // LANES, unfold, 0)


def unfold_call(codes, scales):
    return call(
        unfold_kernel,
        "unfold_states",
        14,
        [HELD] * 2,
        held((STATES, SLOTS, CHANNELS), F32),
        [pltpu.VMEM((SLOTS * STATES, LANES), F32)],
        [codes, scales],
    )


def pool_kernel(*refs):
    pieces, pool, arrived = refs[: 4 * STEPS], refs[-2], refs[-1]
    copies = [
        pltpu.make_async_copy(piece, pool.at[i // 4, pl.ds(i % 4 * 16, 16)], arrived.at[i])
        for i, piece in enumerate(pieces)
    ]
    for copy in copies:
        copy.start()
    for copy in copies:
        copy.wait()


def pool_call(pieces):
    return call(
        pool_kernel,
        "pool_rows",
        50,
        [ANYWHERE] * (4 * STEPS),
        held((STEPS, POOL, GROUP), BF16),
        [pltpu.SemaphoreType.DMA((4 * STEPS,))],
        pieces,
    )


STEP_ROWS, INPUT_ROWS, GATE_ROWS, WINDOW_ROWS = 0, RANK, RANK + ROWS, RANK + 2 * ROWS
TAP_ROW, BIAS_ROW, DECAY_ROW, SKIP_ROW, OFFSET_ROW = 0, 4, 5, 21, 22


def conv_block(inputs, store, fetched, keep, gains, cols):
    past = [
        store[WINDOW_ROWS + k * SLOTS : WINDOW_ROWS + (k + 1) * SLOTS, cols].astype(F32)
        for k in range(3)
    ]
    outs = []
    for tick in range(TICKS):
        rows = slice(tick * SLOTS, (tick + 1) * SLOTS)
        taps = past + [inputs[rows].astype(F32)]
        total = gains[BIAS_ROW : BIAS_ROW + 1, cols]
        for k in range(4):
            total = total + gains[TAP_ROW + k : TAP_ROW + k + 1, cols] * taps[k]
        outs.append(silu(total))
        stays = keep[rows, :1] > 0.5
        past = [jnp.where(stays, taps[k + 1], fetched(k, rows)) for k in range(3)]
    return jnp.concatenate(outs, axis=0), past


def conv_kernel(
    store, onehot, keep, gains, proj, pool, conv_out, terms, scales, taken_out, taken, left, conv_held, gone
):
    copies = []
    total = jnp.zeros((ROWS, TERMS), F32)
    for block in range(STEPS):
        cols = slice(block * CB, (block + 1) * CB)
        fetched = jnp.dot(
            onehot[block // 2], pool[block, :, CODE_LANES:], preferred_element_type=F32
        )
        if block == 0:
            scales[...] = fetched[:, 3 * CB : 3 * CB + LANES]
        for k in range(3):
            taken[block, k] = fetched[:, k * CB : (k + 1) * CB].astype(BF16)
        copies.append(
            pltpu.make_async_copy(taken.at[block], taken_out.at[block], left.at[block])
        )
        copies[-1].start()
        inputs = store[INPUT_ROWS : INPUT_ROWS + ROWS, cols]
        conv, _ = conv_block(
            inputs, store, lambda k, rows: fetched[rows, k * CB : (k + 1) * CB], keep, gains, cols
        )
        conv_held[block] = conv
        copies.append(
            pltpu.make_async_copy(
                conv_held.at[block], conv_out.at[:, pl.ds(block * CB, CB)], gone.at[block]
            )
        )
        copies[-1].start()
        total = total + lax.dot_general(
            conv.astype(BF16), proj[:, cols], (((1,), (1,)), ((), ())), preferred_element_type=F32
        )
    terms[...] = total.astype(BF16)
    for copy in copies:
        copy.wait()


def conv_call(args):
    return call(
        conv_kernel,
        "conv_terms",
        14,
        [HELD] * len(args),
        [
            jax.ShapeDtypeStruct((ROWS, CHANNELS), F32),
            jax.ShapeDtypeStruct((ROWS, TERMS), BF16),
            jax.ShapeDtypeStruct((ROWS, LANES), F32),
            jax.ShapeDtypeStruct((STEPS, 3, ROWS, CB), BF16),
        ],
        [
            pltpu.VMEM((STEPS, 3, ROWS, CB), BF16),
            pltpu.SemaphoreType.DMA((STEPS,)),
            pltpu.VMEM((STEPS, ROWS, CB), F32),
            pltpu.SemaphoreType.DMA((STEPS,)),
        ],
        args,
        [ANYWHERE, HELD, HELD, ANYWHERE],
    )


def project_kernel(
    where,
    s_own,
    s_a,
    s_b,
    s_c,
    gain,
    store,
    keep,
    gains,
    proj,
    taken,
    big,
    conv_out,
    terms,
    win_out,
    values,
    normed,
    entering,
):
    section, column = where[0], where[1]

    @pl.when(section == 0)
    def _():
        entering[...] = store[INPUT_ROWS : INPUT_ROWS + ROWS]

    @pl.when(section == 1)
    def _():
        values[column] = s_own[...]
        values[column ^ 2] = s_a[...]
        values[column ^ 1] = s_b[...]
        values[column ^ 3] = s_c[...]
        total = jnp.zeros((ROWS, 1), F32)
        for f in range(4):
            v = values[f].astype(F32)
            total = total + jnp.sum(v * v, axis=1, keepdims=True)
        factor = lax.rsqrt(total * (1.0 / FEATURES) + 1e-05)
        for f in range(4):
            cols = slice(f * SHARE, (f + 1) * SHARE)
            v = values[f].astype(F32)
            normed[:, cols] = (v * factor * gain[:, cols].astype(F32)).astype(BF16)

    total = jnp.zeros((ROWS, TERMS), F32)
    for block in range(STEPS):
        cols = slice(block * CB, (block + 1) * CB)

        @pl.when(section == 1)
        def _():
            entering[:, cols] = lax.dot_general(
                normed[...], big[cols], (((1,), (1,)), ((), ())), preferred_element_type=F32
            ).astype(BF16)

        conv, past = conv_block(
            entering[:, cols],
            store,
            lambda k, rows: taken[block, k, rows].astype(F32),
            keep,
            gains,
            cols,
        )
        conv_out[:, cols] = conv
        for k in range(3):
            win_out[k, :, cols] = past[k].astype(BF16)
        total = total + lax.dot_general(
            conv.astype(BF16), proj[:, cols], (((1,), (1,)), ((), ())), preferred_element_type=F32
        )
    terms[...] = total.astype(BF16)


def project_call(where, shares, args):
    return call(
        project_kernel,
        "norm_project_conv",
        14,
        [SCALARS] + [HELD] * (4 + len(args)),
        [
            jax.ShapeDtypeStruct((ROWS, CHANNELS), F32),
            jax.ShapeDtypeStruct((ROWS, TERMS), BF16),
            jax.ShapeDtypeStruct((3, SLOTS, CHANNELS), BF16),
        ],
        [
            pltpu.VMEM((4, ROWS, SHARE), BF16),
            pltpu.VMEM((ROWS, FEATURES), BF16),
            pltpu.VMEM((ROWS, CHANNELS), BF16),
        ],
        [where, *shares, *args],
    )


def scan_kernel(final, *refs):
    refs = list(refs)
    take = lambda count: [refs.pop(0) for _ in range(count)]
    (where,) = take(1)
    terms = take(4)
    onehot, keep, cached_scales, pool, conv, start, store, gains = take(8)
    if final:
        scan_out, codes_out, scales_out = take(3)
    else:
        (big,) = take(1)
        kept_out, sent_out = take(2)
    entry, readout, fetched, sizes = take(4)
    if final:
        states, natural, scale_acc = take(3)
    else:
        gated, weight, loaded = take(3)
        parts = [
            pltpu.make_async_copy(
                big.at[pl.ds(b * CB, CB)], weight.at[pl.ds(b * CB, CB)], loaded.at[b]
            )
            for b in range(STEPS)
        ]
        for copy in parts:
            copy.start()
    used = ROWS if final else 2 * SLOTS

    def gate(t, cols):
        first = GATE_ROWS + t * SLOTS
        return store[first : first + SLOTS, cols].astype(F32)

    total = terms[0][...].astype(F32)
    for piece in terms[1:]:
        total = total + piece[...].astype(F32)
    sizes[...] = softplus(
        jnp.dot(
            total[:, :RANK].astype(BF16),
            store[STEP_ROWS : STEP_ROWS + RANK],
            preferred_element_type=F32,
        )
        + gains[OFFSET_ROW : OFFSET_ROW + 1]
    )
    for n in range(STATES):
        e, r = RANK + n, RANK + STATES + n
        entry[n] = jnp.broadcast_to(total[:, e : e + 1], (ROWS, LANES))
        readout[n] = jnp.broadcast_to(total[:, r : r + 1], (ROWS, LANES))
    if final:
        scale_acc[...] = jnp.zeros_like(scale_acc)

    def scan_block(block, carry):
        fetched[...] = jnp.dot(
            onehot[block // 2, :used],
            pool[block, :, :CODE_LANES],
            preferred_element_type=F32,
        )
        for part in range(CB // LANES):
            index = block * (CB // LANES) + part
            scan_tile(index, part)
        return carry

    def scan_tile(index, part):
        cols = tile(index)
        new_scale = column_of(cached_scales[...], index)
        size = [sizes[t * SLOTS : (t + 1) * SLOTS, cols] for t in range(TICKS)]
        conv_now = [conv[t * SLOTS : (t + 1) * SLOTS, cols] for t in range(TICKS)]
        gain = [size[t] * conv_now[t] for t in range(TICKS)]
        total = [gains[SKIP_ROW : SKIP_ROW + 1, cols] * conv_now[t] for t in range(TICKS)]
        arrived_scale = [
            jnp.broadcast_to(new_scale[t * SLOTS : (t + 1) * SLOTS], (SLOTS, LANES))
            for t in range(TICKS - 1)
        ]
        stays = [keep[t * SLOTS : (t + 1) * SLOTS] > 0.5 for t in range(TICKS - 1)]
        square = jnp.zeros((SLOTS, LANES), F32)
        for n in range(STATES):
            rate = gains[DECAY_ROW + n : DECAY_ROW + n + 1, cols] * -LOG2E
            state = start[n, :, cols]
            lanes = slice(n * CB + part * LANES, n * CB + (part + 1) * LANES)
            for t in range(TICKS):
                rows = slice(t * SLOTS, (t + 1) * SLOTS)
                state = jnp.exp2(size[t] * rate) * state + gain[t] * entry[n, rows]
                total[t] = total[t] + readout[n, rows] * state
                if t < TICKS - 1:
                    state = jnp.where(
                        stays[t], state, fetched[rows, lanes] * arrived_scale[t]
                    )
            if final:
                states[n] = state
                square = square + state * state
        if not final:
            for t in range(TICKS):
                rows = slice(t * SLOTS, (t + 1) * SLOTS)
                gated[rows, cols] = (total[t] * silu(gate(t, cols))).astype(BF16)
            return
        for t in range(TICKS):
            scan_out[t * SLOTS : (t + 1) * SLOTS, cols] = total[t].astype(BF16)
        mean = jnp.sum(square, axis=1, keepdims=True) * (1.0 / (STATES * LANES))
        scale = jnp.sqrt(mean + 1e-06).astype(BF16).astype(F32)
        inverse = jnp.broadcast_to(1.0 / scale, (SLOTS, LANES))
        last = slice((TICKS - 1) * SLOTS, TICKS * SLOTS)
        kept = keep[last] > 0.5
        for n in range(STATES):
            lanes = slice(n * CB + part * LANES, n * CB + (part + 1) * LANES)
            natural[pl.ds(n, SLOTS, stride=STATES), :] = jnp.where(
                kept, states[n] * inverse, fetched[last, lanes]
            )
        codes_out[:, :, cols] = natural[...].reshape(SLOTS, STATES, LANES).astype(BF16)
        chosen = jnp.where(kept, jnp.broadcast_to(scale, (SLOTS, LANES)), new_scale[last])
        lane = lax.broadcasted_iota(jnp.int32, (SLOTS, LANES), 1)
        scale_acc[...] = jnp.where(lane == index, chosen, scale_acc[...])

    lax.fori_loop(0, STEPS, scan_block, 0)
    if final:
        scales_out[...] = scale_acc[...].T[: CHANNELS // LANES].astype(BF16)
        return
    for copy in parts:
        copy.wait()
    core = where[1] % 2
    for chip in range(2):
        for offset, out in ((core, kept_out), (1 - core, sent_out)):
            cols = pl.ds(pl.multiple_of((2 * chip + offset) * SHARE, SHARE), SHARE)
            out[chip] = jnp.dot(
                gated[...], weight[:, cols], preferred_element_type=F32
            ).astype(out.dtype)


def scan_call(final, where, terms, args):
    scratch = [
        pltpu.VMEM((STATES, ROWS, LANES), F32),
        pltpu.VMEM((STATES, ROWS, LANES), F32),
        pltpu.VMEM((ROWS if final else 2 * SLOTS, STATES * CB), F32),
        pltpu.VMEM((ROWS, CHANNELS), F32),
    ]
    if final:
        out_shape = [
            jax.ShapeDtypeStruct((ROWS, CHANNELS), BF16),
            jax.ShapeDtypeStruct((SLOTS, STATES, CHANNELS), BF16),
            jax.ShapeDtypeStruct((CHANNELS // LANES, SLOTS), BF16),
        ]
        scratch += [
            pltpu.VMEM((STATES, SLOTS, LANES), F32),
            pltpu.VMEM((SLOTS * STATES, LANES), F32),
            pltpu.VMEM((SLOTS, LANES), F32),
        ]
    else:
        out_shape = [
            jax.ShapeDtypeStruct((2, ROWS, SHARE), F32),
            jax.ShapeDtypeStruct((2, ROWS, SHARE), BF16),
        ]
        scratch += [
            pltpu.VMEM((ROWS, CHANNELS), BF16),
            pltpu.VMEM((CHANNELS, FEATURES), BF16),
            pltpu.SemaphoreType.DMA((STEPS,)),
        ]
    return call(
        functools.partial(scan_kernel, final),
        "scan_final" if final else "scan_gate_project",
        16 if final else 36,
        [SCALARS] + [HELD] * (4 + len(args) - (not final)) + [ANYWHERE] * (not final),
        out_shape,
        scratch,
        [where, *terms, *args],
    )


def chip_kernel(where, kept, got, same, other):
    chip = where[1] // 2
    for place, out in ((chip, same), (1 - chip, other)):
        out[...] = (kept[place] + got[place].astype(F32)).astype(BF16)


def chip_call(where, kept, got):
    share = jax.ShapeDtypeStruct((ROWS, SHARE), BF16)
    return call(
        chip_kernel,
        "sum_on_chip",
        14,
        [SCALARS, HELD, HELD],
        [share, share],
        [],
        [where, kept, got],
    )


def add_kernel(residual, same, other, out):
    total = same[...].astype(F32) + other[...].astype(F32)
    out[...] = (residual[...].astype(F32) + total).astype(BF16)


def add_first_kernel(where, residual, same, other, stream, out):
    @pl.when(where[0] == 0)
    def _():
        add_kernel(residual, same, other, out)

    @pl.when(where[0] == 1)
    def _():
        out[...] = stream[...]


def add_call(kernel, name, args, scalars):
    return call(
        kernel,
        name,
        14,
        [SCALARS] * len(scalars) + [HELD] * len(args),
        [jax.ShapeDtypeStruct((ROWS, SHARE), BF16)],
        [],
        [*scalars, *args],
    )[0]


def exchange(value, step):
    return lax.ppermute(value, "tensor", [(i, i ^ step) for i in range(4)])


def along(value, axis, step):
    if axis == "y":
        pairs = [(i, (i // 4) * 4 + (i + step) % 4) for i in range(16)]
    else:
        pairs = [(i, (i + 4 * step) % 16) for i in range(16)]
    return lax.ppermute(value, "replica", pairs)


def gather_far(first, last, far):
    first_below, last_above = along(first, far, 1), along(last, far, 3)
    last_below, first_above = along(last, far, 1), along(first, far, 3)
    first_far, last_far = along(first_below, far, 1), along(last_above, far, 3)
    return [first, first_below, first_far, first_above, last, last_below, last_far, last_above]


def in_section_one(value, step):
    pairs = [(4 + i, 4 + (i ^ step)) for i in range(4)]
    return lax.ppermute(value, ("section", "tensor"), pairs)


def local(
    inner_input,
    gate_input,
    residual,
    projection,
    state_proj,
    step_proj,
    conv_weight,
    conv_bias,
    decay_rate,
    skip_gain,
    step_bias,
    norm_gain,
    state_codes,
    state_scales,
    conv_window,
    cache_codes,
    cache_scales,
    cache_window,
    finished,
    refill_source,
):
    section = lax.axis_index("section")
    column = lax.axis_index("tensor")
    replica = lax.axis_index("replica")
    where = jnp.stack([section, column, replica // 4, replica % 4]).astype(jnp.int32)

    rows = cache_window.shape[1]
    cached = arrange_call(cache_codes[0], cache_window[0].transpose(1, 0, 2), cache_scales[0])

    near_a = [cached[0]] + [along(cached[0], "y", k) for k in (1, 2, 3)]
    near_b = [cached[1]] + [along(cached[1], "z", k) for k in (1, 2, 3)]
    near_a, near_b, proj = lax.optimization_barrier((near_a, near_b, state_proj[0].T))
    first_a, last_a, first_b, last_b = cat_rows(near_a + near_b)

    sources = lax.dynamic_slice_in_dim(refill_source, replica * SLOTS, SLOTS, 1)
    room = ((0, 0), (0, LANES - ROWS))
    sources = jnp.pad(sources.reshape(1, ROWS), room, constant_values=-1)
    ended = jnp.pad(finished.reshape(1, ROWS), room)

    small = (sources, ended, where, residual.reshape(ROWS, FEATURES), norm_gain[None])
    flat = (
        step_proj[0],
        inner_input.reshape(ROWS, CHANNELS),
        gate_input.reshape(ROWS, CHANNELS),
        conv_window[0].transpose(1, 0, 2).reshape(ROWS, CHANNELS),
    )
    gain_rows = (conv_weight[0], conv_bias, decay_rate[0], skip_gain, step_bias)
    small, flat, codes, weight, gain_rows, first_a = lax.optimization_barrier(
        (small, flat, state_codes[0], projection[0], gain_rows, first_a)
    )
    sources, ended, where, residual_rows, gain = small
    onehot, keep = plan_call(where, sources, ended)
    store = fill_call("hold_store", list(flat))
    states = unfold_call(codes, state_scales[0])
    column_share = lax.dynamic_slice_in_dim(residual_rows, column * SHARE, SHARE, 1)
    pieces = gather_far(first_a, last_a, "z") + gather_far(first_b, last_b, "y")
    gains = jnp.concatenate(gain_rows, axis=0)
    states, store, onehot, keep, gains, pieces = lax.optimization_barrier(
        (states, store, onehot, keep, gains, pieces)
    )
    pool = pool_call(pieces)

    conv_out, terms, cached_scales, taken = conv_call(
        (store, onehot, keep, gains, proj, pool)
    )
    all_terms = [terms] + [exchange(terms, k) for k in (1, 2, 3)]
    shared = (onehot, keep, cached_scales, pool)
    layer = (states, store, gains)
    kept, sent = scan_call(False, where, all_terms, (*shared, conv_out, *layer, weight))

    same, other = chip_call(where, kept, exchange(sent, 1))
    big, same, other = lax.optimization_barrier((weight, same, other))
    big = fill_call("hold_projection", [big])
    other_far = lax.ppermute(other, ("section", "tensor"), [(i, (i + 4) % 8 ^ 2) for i in range(8)])
    same_far = lax.ppermute(same, "section", [(0, 1), (1, 0)])
    big, same_far, other_far = lax.optimization_barrier((big, same_far, other_far))
    stream = add_call(add_kernel, "add_residual", (column_share, same_far, other_far), ())
    other, stream = lax.optimization_barrier((other, stream))
    got_a = in_section_one(stream, 2)
    got_b = in_section_one(stream, 1)
    got_c = in_section_one(got_a, 1)
    other = exchange(other, 2)

    conv_out, terms, window_out = project_call(
        where, (stream, got_a, got_b, got_c), (gain, store, keep, gains, proj, taken, big)
    )
    all_terms = [terms] + [exchange(terms, k) for k in (1, 2, 3)]
    other, conv_out = lax.optimization_barrier((other, conv_out))
    stream = add_call(
        add_first_kernel, "add_first", (column_share, same, other, stream), (where,)
    )
    window_out, stream, conv_out = lax.optimization_barrier(
        (window_out.transpose(1, 0, 2), stream, conv_out)
    )
    scan_out, codes_out, scales_out = scan_call(
        True, where, all_terms, (*shared, conv_out, *layer)
    )
    return (
        stream.reshape(TICKS, SLOTS, SHARE),
        scan_out.reshape(1, TICKS, SLOTS, CHANNELS),
        codes_out[None],
        scales_out.T[None],
        window_out[None],
    )


def solution(mesh):
    return jax.shard_map(
        local,
        mesh=mesh,
        in_specs=(
            P(None, "replica", "tensor"),
            P(None, "replica", "tensor"),
            P(None, "replica", None),
            P("section", "tensor", None),
            P("section", "tensor", None),
            P("section", None, "tensor"),
            P("section", None, "tensor"),
            P("section", "tensor"),
            P("section", None, "tensor"),
            P("section", "tensor"),
            P("section", "tensor"),
            P(),
            P("section", "replica", None, "tensor"),
            P("section", "replica", "tensor"),
            P("section", "replica", None, "tensor"),
            P("section", "replica", None, "tensor"),
            P("section", "replica", "tensor"),
            P("section", "replica", None, "tensor"),
            P(None, "replica"),
            P(),
        ),
        out_specs=(
            P(None, "replica", "tensor"),
            P("section", None, "replica", "tensor"),
            P("section", "replica", None, "tensor"),
            P("section", "replica", "tensor"),
            P("section", "replica", None, "tensor"),
        ),
        check_vma=False,
    )
```
